512 devices in a mesh: space: 32 (over y_hi, z, core), tm: 16 (over y_lo, x).
Axes of the slice: x: 4, y: 8 (y_hi: 2, y_lo: 4; y = y_hi * 4 + y_lo), z: 8, core: 2. Of those that a mesh axis runs over, the one named last changes fastest.
Arguments:
- video_slab: float32 [256, 512, 2048], P('space', None, 'tm'), may hold values from -6 to 6
- first_cols: float32 [512, 160], replicated, may hold values from -0.25 to 0.25
- first_frames: float32 [2048, 160], P('tm'), may hold values from -0.125 to 0.125
- second_rows: float32 [256, 160], P('space'), may hold values from -0.375 to 0.375
- second_frames: float32 [2048, 160], P('tm'), may hold values from -0.125 to 0.125
- third_rows: float32 [256, 96], P('space'), may hold values from -0.375 to 0.375
- third_cols: float32 [512, 96], replicated, may hold values from -0.25 to 0.25
- core_rows: float32 [256, 320], replicated, may hold values from -0.375 to 0.375
- core_cols: float32 [512, 320], replicated, may hold values from -0.25 to 0.25
- core_frames: float32 [2048, 192], P('tm'), may hold values from -0.125 to 0.125
Outputs:
- sketch_rows: float32 [256, 160], P('space')
- sketch_cols: float32 [512, 160], P('space')
- sketch_frames: float32 [2048, 96], P('tm')
- core_sketch: float32 [320, 320, 192], P(None, 'space', 'tm')
The draws below stay inside these ranges and needn't reach their ends.
All inputs are finite; a program needn't handle non-finite values.
Results may differ from the reference program's by a relative error of at most 0.0001.
Values sent between devices are 32-bit elements; how exact they have to be, the bound alone decides.
A program may use at most 64 MiB of HBM per device.

```python
import jax
import jax.numpy as jnp
from jax import lax

COLS = 512
FRAMES_DEV = 128
RANK_ROW = 160
RANK_COL = 160
RANK_FRAME = 96
CORE_ROW = 320
CORE_COL = 320
CORE_FRAME = 192
ROWS = 256
FRAMES = 2048


def spiked(entries, key, source, target, blocks, factor):
    owner, partner = [(jnp.arange(entries.shape[position]) // (entries.shape[position] // blocks)).reshape([-1 if axis == position else 1 for axis in range(entries.ndim)]) for position in (source, target)]
    chosen = jax.random.permutation(key, blocks)[partner]
    strong = (owner == chosen) | (owner == (partner + blocks // 2) % blocks)
    return jnp.where(strong, factor * entries, entries)


def block_levels(key, extent, split, low, largest):
    def one(position, shards_of):
        heights = jax.random.uniform(jax.random.fold_in(jax.random.fold_in(key, 6), position), (shards_of,), jnp.float32, low / len(split), largest / len(split))
        return jnp.repeat(jnp.exp(heights), extent[position] // shards_of).reshape((-1,) + (1,) * (len(extent) - position - 1))

    loudness = one(*split[0])
    for cut in split[1:]:
        loudness = loudness * one(*cut)
    return loudness


def normal_values(own_key, shape, width, reach, shards=(), kind=jnp.bfloat16):
    array = width * jax.random.normal(own_key, shape, jnp.float32)
    if shards:
        array = array * block_levels(own_key, shape, shards, -0.22, 0.18)
    return jnp.clip(array, -reach, reach).astype(kind)


def gaussian_with(key, dims, width, most, split, heavy, dtype=jnp.bfloat16):
    values = width * jax.random.normal(key, dims, jnp.float32)
    if split:
        values = values * block_levels(key, dims, split, -0.22, 0.18)
    return jnp.clip(spiked(values, jax.random.fold_in(key, 3), *heavy), -most, most).astype(dtype)


def setup_inputs(seed: int = 0) -> dict:
    key_of = jax.random.split(jax.random.key(seed), 11)
    video_slab = gaussian_with(key_of[0], (ROWS, COLS, FRAMES), 1.0, 6.0, ((0, 32), (2, 16)), (0, 1, 32, 2.75), jnp.float32)
    first_cols = normal_values(key_of[1], (COLS, RANK_ROW), COLS ** -0.5, 0.25, (), jnp.float32)
    first_frames = normal_values(key_of[2], (FRAMES, RANK_ROW), FRAMES ** -0.5, 0.125, ((0, 16),), jnp.float32)
    second_rows = normal_values(key_of[3], (ROWS, RANK_COL), ROWS ** -0.5, 0.375, ((0, 32),), jnp.float32)
    second_frames = normal_values(key_of[4], (FRAMES, RANK_COL), FRAMES ** -0.5, 0.125, ((0, 16),), jnp.float32)
    third_rows = normal_values(key_of[5], (ROWS, RANK_FRAME), ROWS ** -0.5, 0.375, ((0, 32),), jnp.float32)
    third_cols = normal_values(key_of[6], (COLS, RANK_FRAME), COLS ** -0.5, 0.25, (), jnp.float32)
    core_rows = normal_values(key_of[7], (ROWS, CORE_ROW), ROWS ** -0.5, 0.375, (), jnp.float32)
    core_cols = normal_values(key_of[8], (COLS, CORE_COL), COLS ** -0.5, 0.25, (), jnp.float32)
    core_frames = normal_values(key_of[9], (FRAMES, CORE_FRAME), FRAMES ** -0.5, 0.125, ((0, 16),), jnp.float32)
    return {"video_slab": video_slab, "first_cols": first_cols, "first_frames": first_frames, "second_rows": second_rows, "second_frames": second_frames, "third_rows": third_rows, "third_cols": third_cols, "core_rows": core_rows, "core_cols": core_cols, "core_frames": core_frames}


highest = lax.Precision.HIGHEST


def reference(video_slab, first_cols, first_frames, second_rows, second_frames, third_rows, third_cols, core_rows, core_cols, core_frames):
    blocks = FRAMES // FRAMES_DEV

    def step(index, carry):
        rows_acc, cols_acc, frames_acc, core_acc = carry
        start = (index * FRAMES_DEV).astype(jnp.int32)
        block = lax.dynamic_slice_in_dim(video_slab, start, FRAMES_DEV, 2)
        frames_one = lax.dynamic_slice_in_dim(first_frames, start, FRAMES_DEV, 0)
        frames_two = lax.dynamic_slice_in_dim(second_frames, start, FRAMES_DEV, 0)
        frames_core = lax.dynamic_slice_in_dim(core_frames, start, FRAMES_DEV, 0)
        first_part = jnp.einsum('ijt,jr->itr', block, first_cols, precision=highest)
        rows_acc = rows_acc + jnp.einsum('itr,tr->ir', first_part, frames_one, precision=highest)
        second_part = jnp.einsum('ijt,tr->ijr', block, frames_two, precision=highest)
        cols_acc = cols_acc + jnp.einsum('ijr,ir->jr', second_part, second_rows, precision=highest)
        third_part = jnp.einsum('ijt,jr->itr', block, third_cols, precision=highest)
        frame_block = jnp.einsum('itr,ir->tr', third_part, third_rows, precision=highest)
        frames_acc = lax.dynamic_update_slice_in_dim(frames_acc, frame_block, start, 0)
        core_part = jnp.einsum('ijt,jb->itb', block, core_cols, precision=highest)
        core_part = jnp.einsum('itb,ia->atb', core_part, core_rows, precision=highest)
        core_acc = core_acc + jnp.einsum('atb,tc->abc', core_part, frames_core, precision=highest)
        return rows_acc, cols_acc, frames_acc, core_acc

    start_carry = (jnp.zeros((ROWS, RANK_ROW), jnp.float32), jnp.zeros((COLS, RANK_COL), jnp.float32),
                   jnp.zeros((FRAMES, RANK_FRAME), jnp.float32), jnp.zeros((CORE_ROW, CORE_COL, CORE_FRAME), jnp.float32))
    sketch_rows, sketch_cols, sketch_frames, core_sketch = lax.fori_loop(0, blocks, step, start_carry)
    return sketch_rows, sketch_cols, sketch_frames, core_sketch
```

```python
import functools

import jax
import jax.numpy as jnp
from jax import lax
from jax.experimental import pallas as pl
from jax.experimental.pallas import tpu as pltpu
from jax.sharding import PartitionSpec as P

MESH = pl.DeviceIdType.MESH
f32, bf16 = jnp.float32, jnp.bfloat16

NN = (((1,), (0,)), ((), ()))
NT = (((1,), (1,)), ((), ()))
TN = (((0,), (0,)), ((), ()))


def dot(a, b, dims=NN):
    return lax.dot_general(a, b, dims, preferred_element_type=f32)


def halves(a):
    high = a.astype(bf16)
    return high, (a - high.astype(f32)).astype(bf16)


def kernel(
    slab_given, first_cols_given, third_cols_given, core_cols_given, first_frames_given, second_frames_given,
    core_frames_given, second_rows_given, third_rows_given, core_rows_given,
    out_rows, out_cols, out_frames, out_core,
    slab, first_cols, third_cols, core_cols, first_frames, second_frames, core_frames, second_rows, third_rows, core_rows,
    order, cols_hi, cols_lo, frames_hi, frames_lo, rows_hi, rows_lo, split, inner, folded_hi, folded_lo, second_hi, second_lo, third_wide,
    part, far, near, after, pair_in, cross_in, tiles, gathered,
    small, core_in, layer_out, layer_in, frame_part, frame_in, frame_layer, frame_other, frame_last,
    line_out, line_in, ring_out, ring_in,
    load_sem, send_sem, recv_sem, send_space, recv_space, send_layer, recv_layer, send_line, recv_line, send_ring, recv_ring,
):
    space, tm = lax.axis_index("space"), lax.axis_index("tm")
    y_hi, z, core = space // 16, lax.rem(space // 2, 8), lax.rem(space, 2)
    y_lo, x = tm // 4, lax.rem(tm, 4)
    y = y_hi * 4 + y_lo

    def at_x(other):
        return (space, y_lo * 4 + other)

    def at_y(other):
        return (lax.rem(other // 4, 2) * 16 + z * 2 + core, lax.rem(other, 4) * 4 + x)

    def at_z(other):
        return (y_hi * 16 + other * 2 + core, tm)

    def load(number, source, target):
        return pltpu.make_async_copy(source, target, load_sem.at[number])

    def load_pair(pair):
        rows = pl.ds(2 * pair, 2)
        return load(pair, slab_given.at[rows], slab.at[rows])

    loads = {
        "core_cols": load(4, core_cols_given, core_cols),
        "first_cols": load(5, first_cols_given, first_cols),
        "third_cols": load(6, third_cols_given, third_cols),
        "core_frames": load(7, core_frames_given, core_frames),
        "second_rows": load(8, second_rows_given, second_rows),
        "third_rows": load(9, third_rows_given, third_rows),
        "second_frames": load(10, second_frames_given, second_frames),
        "first_frames": load(11, first_frames_given, first_frames),
        "core_rows": load(12, core_rows_given, core_rows),
    }
    for each in ("core_cols", "first_cols", "third_cols"):
        loads[each].start()
    for pair in range(4):
        load_pair(pair).start()
    for each in ("core_frames", "second_rows", "third_rows", "second_frames", "first_frames", "core_rows"):
        loads[each].start()

    barrier = pltpu.get_barrier_semaphore()

    def greet(device):
        pl.semaphore_signal(barrier, inc=1, device_id=device, device_id_type=MESH)

    @pl.loop(1, 32)
    def _(step):
        greet((lax.rem(space + step, 32), tm))

    for step in (1, 2, 3):
        greet(at_x(lax.rem(x + step, 4)))
        for flip in (0, 16):
            greet((lax.rem(space + flip, 32), lax.rem(y_lo + step, 4) * 4 + x))

    loads["core_cols"].wait()
    loads["first_cols"].wait()
    loads["third_cols"].wait()
    loads["core_frames"].wait()
    hi, lo = halves(first_cols[...])
    cols_hi[0:160, :], cols_lo[0:160, :] = hi, lo
    hi, lo = halves(third_cols[...])
    cols_hi[160:256, :], cols_lo[160:256, :] = hi, lo
    for quarter in range(4):
        lanes = slice(128 * quarter, 128 * quarter + 128)
        order[quarter] = core_cols[:, lanes]
        for place in range(10):
            hi, lo = halves(order[quarter, pl.ds(place, 32, stride=10), :])
            rows = slice(256 + 32 * place, 288 + 32 * place)
            cols_hi[rows, lanes], cols_lo[rows, lanes] = hi, lo

    for other in range(4):
        for place in range(4):
            line = (place % 2) * 2 + place // 2
            base = 12 * (line * 4 + other)
            row = 24 * (other * 4 + place)
            eight = core_frames[base : base + 8, :]
            four = core_frames[base + 8 : base + 12, :]
            blank = jnp.zeros((8, 128), f32)
            blank4 = jnp.zeros((4, 128), f32)
            block = jnp.concatenate(
                [
                    jnp.concatenate([eight, blank], axis=1),
                    jnp.concatenate([blank, eight], axis=1),
                    jnp.concatenate([four, blank4], axis=1),
                    jnp.concatenate([blank4, four], axis=1),
                ],
                axis=0,
            )
            hi, lo = halves(block)
            frames_hi[row : row + 24, :], frames_lo[row : row + 24, :] = hi, lo

    def columns(pair):
        load_pair(pair).wait()
        lanes = pl.ds(pl.multiple_of(pair * 256, 256), 256)
        low_lanes = pl.ds(pl.multiple_of(pair * 256 + 1024, 256), 256)
        block = jnp.concatenate([slab[2 * pair], slab[2 * pair + 1]], axis=1)
        hi, lo = halves(block)
        split[:, lanes] = hi
        split[:, low_lanes] = lo
        product = dot(cols_hi[...], hi) + dot(cols_hi[...], lo) + dot(cols_lo[...], hi)
        inner[pair] = product[0:256, :]
        hi, lo = halves(product[256:576, :].reshape(2, 5, 32, 256))
        chunk = pair // 2
        for row in range(2):
            place = 2 * lax.rem(pair, 2) + row
            for half in range(2):
                folded_hi[chunk, :, place, :, half * 128 : half * 128 + 128] = hi[half, :, :, row * 128 : row * 128 + 128]
                folded_lo[chunk, :, place, :, half * 128 : half * 128 + 128] = lo[half, :, :, row * 128 : row * 128 + 128]

    def frames(chunk):
        right_hi = folded_hi[chunk].reshape(640, 256)
        right_lo = folded_lo[chunk].reshape(640, 256)
        product = (
            dot(frames_hi[...], right_hi, NT) + dot(frames_hi[...], right_lo, NT) + dot(frames_lo[...], right_hi, NT)
        )
        part[chunk] = product.reshape(4, 2, 2, 24, 640)

    def copy(source, target, number, device):
        return pltpu.make_async_remote_copy(
            src_ref=source, dst_ref=target, send_sem=send_sem.at[number], recv_sem=recv_sem.at[number],
            device_id=device, device_id_type=MESH,
        )

    right, left, across = lax.rem(x + 1, 4), lax.rem(x + 3, 4), lax.rem(x + 2, 4)
    ways = ((right, left), (left, right))

    @pl.loop(0, 2)
    def _(pair):
        columns(pair)

    frames(0)
    pl.semaphore_wait(barrier, 40)
    sent = []

    def begin(chunk):
        onward, back = ways[chunk]
        first = copy(part.at[chunk, across], far.at[chunk], 3 * chunk, at_x(onward))
        second = copy(part.at[chunk, back], near.at[chunk], 3 * chunk + 1, at_x(back))
        first.start()
        second.start()
        sent.extend([first, second])
        return first, second

    def relay(chunk, first):
        onward, _ = ways[chunk]
        first.wait_recv()
        part[chunk, onward] += far[chunk]
        third = copy(part.at[chunk, onward], after.at[chunk], 3 * chunk + 2, at_x(onward))
        third.start()
        sent.append(third)
        return third

    ring = [begin(0)]

    @pl.loop(2, 4)
    def _(pair):
        columns(pair)

    frames(1)
    ring.append(begin(1))

    index_k = lax.broadcasted_iota(jnp.int32, (8, 1024), 0)
    index_l = lax.broadcasted_iota(jnp.int32, (8, 1024), 1) // 128
    spread = (index_k == index_l).astype(f32)

    for each in ("second_rows", "third_rows", "second_frames", "first_frames", "core_rows"):
        loads[each].wait()

    def widen(values):
        return lax.dot_general(values, spread, TN, precision=lax.Precision.HIGHEST, preferred_element_type=f32)

    wide_second = widen(second_rows[...])
    for row in range(8):
        lanes = slice(row * 128, row * 128 + 128)
        value = second_frames[...] * wide_second[:, lanes]
        hi, lo = halves(value)
        second_hi[0:128, lanes], second_lo[0:128, lanes] = hi[0:128], lo[0:128]
        for copies in range(4):
            rows = slice(128 + 32 * copies, 160 + 32 * copies)
            second_hi[rows, lanes], second_lo[rows, lanes] = hi[128:160], lo[128:160]
    third_wide[...] = widen(third_rows[...])

    relayed = [relay(0, ring[0][0])]

    second = (
        dot(split[:, 0:1024], second_hi[...], NT)
        + dot(split[:, 1024:2048], second_hi[...], NT)
        + dot(split[:, 0:1024], second_lo[...], NT)
    )
    main = second[:, 0:128].reshape(2, 8, 2, 16, 128)
    tail = second[:, 128:256].reshape(2, 8, 2, 2, 8, 128)
    quarter = lax.broadcasted_iota(jnp.int32, (8, 8, 128), 2) // 32
    for which in range(2):
        small[which, :, 0:16, :] = main[0, :, which]
        small[which, :, 16:32, :] = main[1, :, which]
        small[which, :, 32:40, :] = jnp.where(
            quarter < 2,
            jnp.where(quarter == 0, tail[0, :, which, 0], tail[0, :, which, 1]),
            jnp.where(quarter == 2, tail[1, :, which, 0], tail[1, :, which, 1]),
        )

    total = jnp.zeros((96, 128), f32)
    for row in range(8):
        place = slice((row % 2) * 128, (row % 2) * 128 + 128)
        total = total + inner[row // 2, 160:256, place] * third_wide[:, row * 128 : row * 128 + 128]
    frame_part[...] = total.reshape(2, 48, 128)

    other_core = (y_hi * 16 + z * 2 + 1 - core, tm)
    swap = copy(small.at[1 - core], core_in, 6, other_core)
    swap.start()
    swap_frames = copy(frame_part.at[1 - core], frame_in, 7, other_core)
    swap_frames.start()
    sent.extend([swap, swap_frames])

    relayed.append(relay(1, ring[1][0]))

    rows_total = jnp.zeros((16, 160), f32)
    index_k = lax.broadcasted_iota(jnp.int32, (16, 256), 0)
    index_l = lax.broadcasted_iota(jnp.int32, (16, 256), 1) // 128
    for pair in range(4):
        value = inner[pair, 0:160, :] * jnp.concatenate([first_frames[...], first_frames[...]], axis=1)
        hi, lo = halves(value)
        ones = (index_k == index_l + 2 * pair).astype(f32).astype(bf16)
        rows_total = rows_total + dot(ones, hi, NT) + dot(ones, lo, NT)

    hi, lo = halves(core_rows[...])
    rows_hi[...], rows_lo[...] = hi, lo

    swap.wait_recv()
    layer_out[...] = small[core] + core_in[...]
    swap_frames.wait_recv()
    frame_layer[z] = frame_part[core] + frame_in[...]

    def layer_copy(other, slot, kind):
        if kind == 0:
            source, target = layer_out.at[other], layer_in.at[slot]
        else:
            source, target = frame_layer.at[z], frame_layer.at[slot]
        return pltpu.make_async_remote_copy(
            src_ref=source, dst_ref=target, send_sem=send_layer.at[kind, other], recv_sem=recv_layer.at[kind, slot],
            device_id=at_z(other), device_id_type=MESH,
        )

    @pl.loop(1, 8)
    def _(step):
        other = lax.rem(z + step, 8)
        layer_copy(other, z, 0).start()
        layer_copy(other, z, 1).start()

    layer_in[z] = layer_out[z]

    def pair_stage(chunk):
        ring[chunk][1].wait_recv()
        relayed[chunk].wait_recv()
        part[chunk, x] = part[chunk, x] + near[chunk] + after[chunk]
        step = copy(
            part.at[chunk, x, 1 - lax.rem(y_lo, 2)], pair_in.at[chunk], 8 + chunk,
            (space, (y_lo + 1 - 2 * lax.rem(y_lo, 2)) * 4 + x),
        )
        step.start()
        sent.append(step)
        return step

    def cross_stage(chunk, step):
        step.wait_recv()
        mine = lax.rem(y_lo, 2)
        part[chunk, x, mine] = part[chunk, x, mine] + pair_in[chunk]
        cross = copy(
            part.at[chunk, x, mine, 1 - y_lo // 2], cross_in.at[chunk], 10 + chunk,
            (space, lax.rem(y_lo + 2, 4) * 4 + x),
        )
        cross.start()
        sent.append(cross)
        return cross

    pairs = [pair_stage(0)]

    @pl.loop(1, 8)
    def _(step):
        other = lax.rem(z + step, 8)
        layer_copy(other, other, 0).wait_recv()
        layer_copy(other, other, 1).wait_recv()

    line_out[0:40, :] = jnp.sum(layer_in[...], axis=0)
    line_out[40:48, :] = rows_total[0:8, 0:128]
    line_out[48:56, :] = jnp.concatenate([rows_total[0:8, 128:160], jnp.zeros((8, 96), f32)], axis=1)
    frame_other[...] = jnp.sum(frame_layer[...], axis=0)

    def line_copy(other, slot):
        return pltpu.make_async_remote_copy(
            src_ref=line_out, dst_ref=line_in.at[slot], send_sem=send_line.at[other], recv_sem=recv_line.at[slot],
            device_id=at_x(other), device_id_type=MESH,
        )

    for step in (1, 2, 3):
        line_copy(lax.rem(x + step, 4), x).start()
    line_in[x] = line_out[...]
    flip = copy(frame_other, frame_last, 12, (lax.rem(space + 16, 32), tm))
    flip.start()
    sent.append(flip)

    pairs.append(pair_stage(1))
    crosses = [cross_stage(0, pairs[0])]

    for step in (1, 2, 3):
        other = lax.rem(x + step, 4)
        line_copy(other, other).wait_recv()
    summed = jnp.sum(line_in[...], axis=0)
    for half in range(2):
        ring_out[half, 0:16, :] = summed[16 * half : 16 * half + 16]
        ring_out[half, 16:40, :] = summed[32:56]

    def ring_copy(other, slot):
        return pltpu.make_async_remote_copy(
            src_ref=ring_out.at[other // 4], dst_ref=ring_in.at[slot], send_sem=send_ring.at[other], recv_sem=recv_ring.at[slot],
            device_id=at_y(other), device_id_type=MESH,
        )

    @pl.loop(1, 8)
    def _(step):
        ring_copy(lax.rem(y + step, 8), y).start()

    ring_in[y] = ring_out[y_hi]
    crosses.append(cross_stage(1, pairs[1]))

    flip.wait_recv()
    frame_in_place = frame_other[...] + frame_last[...]
    out_frames[core] = frame_in_place
    swap_back = copy(out_frames.at[core], out_frames.at[core], 13, other_core)
    swap_back.start()
    sent.append(swap_back)

    for chunk in range(2):
        crosses[chunk].wait_recv()
        value = part[chunk, x, lax.rem(y_lo, 2), y_lo // 2] + cross_in[chunk]
        stacked = jnp.concatenate(
            [value[:, 128 * group : 128 * group + 128] for group in range(5)] + [jnp.zeros((8, 128), f32)], axis=0
        )
        turned = stacked.T
        for place in range(4):
            tiles[pl.ds(4 * chunk + place, 32, stride=8), :] = turned[32 * place : 32 * place + 32, :]

    def tile_copy(other, slot):
        return pltpu.make_async_remote_copy(
            src_ref=tiles.at[pl.ds(pl.multiple_of(other * 8, 8), 8), :],
            dst_ref=gathered.at[pl.ds(pl.multiple_of(slot * 8, 8), 8), :],
            send_sem=send_space.at[other], recv_sem=recv_space.at[slot],
            device_id=(other, tm), device_id_type=MESH,
        )

    @pl.loop(1, 32)
    def _(step):
        tile_copy(lax.rem(space + step, 32), space).start()

    own = pl.ds(pl.multiple_of(space * 8, 8), 8)
    gathered[own, :] = tiles[own, :]

    @pl.loop(1, 8)
    def _(step):
        other = lax.rem(y + step, 8)
        ring_copy(other, other).wait_recv()

    final = jnp.sum(ring_in[:, 0:24, :], axis=0)
    own_rows = jnp.sum(ring_in[pl.ds(y_hi * 4, 4), 24:40, :], axis=0)
    out_rows[:, 0:128] = own_rows[0:8]
    out_rows[:, 128:160] = own_rows[8:16, 0:32]
    out_cols[:, 0:128] = final[0:16]
    for half in range(2):
        out_cols[8 * half : 8 * half + 8, 128:160] = jnp.where(
            y_hi == 0, final[16:24, 32 * half : 32 * half + 32], final[16:24, 64 + 32 * half : 96 + 32 * half]
        )

    @pl.loop(1, 32)
    def _(step):
        other = lax.rem(space + step, 32)
        tile_copy(other, other).wait_recv()

    hi, lo = halves(gathered[...].T)
    result = dot(hi, rows_hi[...], NT) + dot(hi, rows_lo[...], NT) + dot(lo, rows_hi[...], NT)
    for group in range(5):
        for half in range(2):
            base = 24 * group
            out_core[half * 5 + group, 0:8, :] = result[base + 8 * half : base + 8 * half + 8]
            out_core[half * 5 + group, 8:12, :] = result[base + 16 + 4 * half : base + 20 + 4 * half]

    swap_back.wait_recv()
    for each in sent:
        each.wait_send()

    @pl.loop(1, 8)
    def _(step):
        other = lax.rem(z + step, 8)
        layer_copy(other, z, 0).wait_send()
        layer_copy(other, z, 1).wait_send()
        ring_copy(lax.rem(y + step, 8), y).wait_send()

    for step in (1, 2, 3):
        line_copy(lax.rem(x + step, 4), x).wait_send()

    @pl.loop(1, 32)
    def _(step):
        tile_copy(lax.rem(space + step, 32), space).wait_send()


def per_device(
    video_slab, first_cols, first_frames, second_rows, second_frames, third_rows, third_cols, core_rows, core_cols, core_frames,
):
    arguments = (
        video_slab, first_cols.T, third_cols.T, core_cols.T, first_frames.T, second_frames.T, core_frames.T,
        second_rows, third_rows, core_rows.T,
    )
    vmem = pl.BlockSpec(memory_space=pltpu.VMEM)
    dma = pltpu.SemaphoreType.DMA
    scratch = [pltpu.VMEM(each.shape, f32) for each in arguments] + [
        pltpu.VMEM((4, 320, 128), f32),
        pltpu.VMEM((576, 512), bf16), pltpu.VMEM((576, 512), bf16),
        pltpu.VMEM((384, 256), bf16), pltpu.VMEM((384, 256), bf16),
        pltpu.VMEM((320, 256), bf16), pltpu.VMEM((320, 256), bf16),
        pltpu.VMEM((512, 2048), bf16),
        pltpu.VMEM((4, 256, 256), f32),
        pltpu.VMEM((2, 5, 4, 32, 256), bf16), pltpu.VMEM((2, 5, 4, 32, 256), bf16),
        pltpu.VMEM((256, 1024), bf16), pltpu.VMEM((256, 1024), bf16),
        pltpu.VMEM((96, 1024), f32),
        pltpu.VMEM((2, 4, 2, 2, 24, 640), f32),
        pltpu.VMEM((2, 2, 2, 24, 640), f32), pltpu.VMEM((2, 2, 2, 24, 640), f32), pltpu.VMEM((2, 2, 2, 24, 640), f32),
        pltpu.VMEM((2, 2, 24, 640), f32),
        pltpu.VMEM((2, 24, 640), f32),
        pltpu.VMEM((256, 128), f32), pltpu.VMEM((256, 128), f32),
        pltpu.VMEM((2, 8, 40, 128), f32), pltpu.VMEM((8, 40, 128), f32),
        pltpu.VMEM((8, 40, 128), f32), pltpu.VMEM((8, 40, 128), f32),
        pltpu.VMEM((2, 48, 128), f32), pltpu.VMEM((48, 128), f32), pltpu.VMEM((8, 48, 128), f32),
        pltpu.VMEM((48, 128), f32), pltpu.VMEM((48, 128), f32),
        pltpu.VMEM((56, 128), f32), pltpu.VMEM((4, 56, 128), f32),
        pltpu.VMEM((2, 40, 128), f32), pltpu.VMEM((8, 40, 128), f32),
        dma((13,)), dma((14,)), dma((14,)), dma((32,)), dma((32,)), dma((2, 8)), dma((2, 8)), dma((4,)), dma((4,)), dma((8,)), dma((8,)),
    ]
    rows, cols, frames, core = pl.pallas_call(
        kernel,
        out_shape=[
            jax.ShapeDtypeStruct((8, 160), f32),
            jax.ShapeDtypeStruct((16, 160), f32),
            jax.ShapeDtypeStruct((2, 48, 128), f32),
            jax.ShapeDtypeStruct((10, 12, 320), f32),
        ],
        in_specs=[pl.BlockSpec(memory_space=pltpu.HBM)] * 10,
        out_specs=[vmem] * 4,
        scratch_shapes=scratch,
        compiler_params=pltpu.CompilerParams(collective_id=0, has_side_effects=True, vmem_limit_bytes=60 * 2**20),
    )(*arguments)
    return rows, cols, frames.reshape(96, 128).T, core.transpose(2, 0, 1)


def solution(mesh):
    return jax.shard_map(
        per_device,
        mesh=mesh,
        in_specs=(
            P("space", None, "tm"),
            P(),
            P("tm", None),
            P("space", None),
            P("tm", None),
            P("space", None),
            P(),
            P(),
            P(),
            P("tm", None),
        ),
        out_specs=(P("space", None), P("space", None), P("tm", None), P(None, "space", "tm")),
        check_vma=False,
    )
```

```python
import functools

import jax
import jax.numpy as jnp
from jax import lax
from jax.experimental import pallas as pl
from jax.experimental.pallas import tpu as pltpu
from jax.sharding import PartitionSpec as P

MESH = pl.DeviceIdType.MESH
f32, bf16 = jnp.float32, jnp.bfloat16

NN = (((1,), (0,)), ((), ()))
NT = (((1,), (1,)), ((), ()))
TN = (((0,), (0,)), ((), ()))


def dot(a, b, dims=NN):
    return lax.dot_general(a, b, dims, preferred_element_type=f32)


def halves(a):
    high = a.astype(bf16)
    return high, (a - high.astype(f32)).astype(bf16)


def kernel(
    slab_given, first_cols_given, third_cols_given, core_cols_given, first_frames_given, second_frames_given,
    core_frames_given, second_rows_given, third_rows_given,
    gathered, out_small, out_frames,
    slab, first_cols, third_cols, core_cols, first_frames, second_frames, core_frames, second_rows, third_rows,
    order, cols_hi, cols_lo, frames_hi, frames_lo, split, inner, rest_hi, rest_lo, second_hi, second_lo, third_wide,
    part, far, near, after, line, tiles,
    small, core_in, layer_out, layer_in, frame_part, frame_in, frame_layer, frame_other, frame_last,
    line_out, line_in, ring_out, ring_in,
    load_sem, send_sem, recv_sem, send_space, recv_space, send_layer, recv_layer, send_line, recv_line, send_ring, recv_ring, send_y, recv_y,
):
    space, tm = lax.axis_index("space"), lax.axis_index("tm")
    y_hi, z, core = space // 16, lax.rem(space // 2, 8), lax.rem(space, 2)
    y_lo, x = tm // 4, lax.rem(tm, 4)
    y = y_hi * 4 + y_lo

    def at_x(other):
        return (space, y_lo * 4 + other)

    def at_y(other):
        return (lax.rem(other // 4, 2) * 16 + z * 2 + core, lax.rem(other, 4) * 4 + x)

    def at_z(other):
        return (y_hi * 16 + other * 2 + core, tm)

    def load(number, source, target):
        return pltpu.make_async_copy(source, target, load_sem.at[number])

    def load_pair(pair):
        rows = pl.ds(2 * pair, 2)
        return load(pair, slab_given.at[rows], slab.at[rows])

    loads = {
        "core_cols": load(4, core_cols_given, core_cols),
        "first_cols": load(5, first_cols_given, first_cols),
        "third_cols": load(6, third_cols_given, third_cols),
        "core_frames": load(7, core_frames_given, core_frames),
        "second_rows": load(8, second_rows_given, second_rows),
        "third_rows": load(9, third_rows_given, third_rows),
        "second_frames": load(10, second_frames_given, second_frames),
        "first_frames": load(11, first_frames_given, first_frames),
    }
    for each in ("core_cols", "core_frames", "first_cols", "third_cols"):
        loads[each].start()
    for pair in range(4):
        load_pair(pair).start()
    for each in ("second_rows", "third_rows", "second_frames", "first_frames"):
        loads[each].start()

    barrier = pltpu.get_barrier_semaphore()

    def greet(device):
        pl.semaphore_signal(barrier, inc=1, device_id=device, device_id_type=MESH)

    @pl.loop(1, 16)
    def _(step):
        greet((y_hi * 16 + lax.rem(space + step, 16), tm))

    @pl.loop(1, 8)
    def _(step):
        greet(at_y(lax.rem(y + step, 8)))

    for step in (1, 2, 3):
        greet(at_x(lax.rem(x + step, 4)))

    loads["core_cols"].wait()
    loads["first_cols"].wait()
    loads["third_cols"].wait()
    loads["core_frames"].wait()
    hi, lo = halves(first_cols[...])
    cols_hi[0:160, :], cols_lo[0:160, :] = hi, lo
    hi, lo = halves(third_cols[...])
    cols_hi[160:256, :], cols_lo[160:256, :] = hi, lo
    for quarter in range(4):
        lanes = slice(128 * quarter, 128 * quarter + 128)
        order[quarter] = core_cols[:, lanes]
        for half in range(2):
            for place in range(10):
                hi, lo = halves(order[quarter, pl.ds(160 * half + place, 16, stride=10), :])
                base = 256 + 128 * half + 16 * place if place < 8 else 512 + 32 * half + 16 * (place - 8)
                cols_hi[base : base + 16, lanes], cols_lo[base : base + 16, lanes] = hi, lo

    for other in range(4):
        for place in range(4):
            base = 12 * (place * 4 + other)
            row = 24 * (other * 4 + place)
            eight = core_frames[base : base + 8, :]
            four = core_frames[base + 8 : base + 12, :]
            blank = jnp.zeros((8, 128), f32)
            blank4 = jnp.zeros((4, 128), f32)
            block = jnp.concatenate(
                [
                    jnp.concatenate([eight, blank], axis=1),
                    jnp.concatenate([blank, eight], axis=1),
                    jnp.concatenate([four, blank4], axis=1),
                    jnp.concatenate([blank4, four], axis=1),
                ],
                axis=0,
            )
            hi, lo = halves(block)
            frames_hi[row : row + 24, :], frames_lo[row : row + 24, :] = hi, lo

    def columns(pair):
        load_pair(pair).wait()
        lanes = pl.ds(pl.multiple_of(pair * 256, 256), 256)
        low_lanes = pl.ds(pl.multiple_of(pair * 256 + 1024, 256), 256)
        block = jnp.concatenate([slab[2 * pair], slab[2 * pair + 1]], axis=1)
        hi, lo = halves(block)
        split[:, lanes] = hi
        split[:, low_lanes] = lo
        product = dot(cols_hi[...], hi) + dot(cols_hi[...], lo) + dot(cols_lo[...], hi)
        inner[pair] = product[0:256, :]
        hi, lo = halves(product[512:576, :].reshape(2, 32, 256))
        rest_hi[:, pair], rest_lo[:, pair] = hi, lo
        frames(pair, *halves(product[256:512, :]))

    def frames(unit, right_hi, right_lo):
        product = (
            dot(frames_hi[...], right_hi, NT) + dot(frames_hi[...], right_lo, NT) + dot(frames_lo[...], right_hi, NT)
        )
        for half in range(2):
            part[unit, :, half] = product[:, 128 * half : 128 * half + 128].reshape(4, 4, 24, 128)

    def copy(source, target, number, device):
        return pltpu.make_async_remote_copy(
            src_ref=source, dst_ref=target, send_sem=send_sem.at[number], recv_sem=recv_sem.at[number],
            device_id=device, device_id_type=MESH,
        )

    right, left, across = lax.rem(x + 1, 4), lax.rem(x + 3, 4), lax.rem(x + 2, 4)

    sent = []

    ways = ((right, left), (left, right), (right, left), (left, right), (right, left))

    def far_copy(unit):
        return copy(part.at[unit, across], far.at[unit], 3 * unit, at_x(ways[unit][0] if unit < 4 else across))

    def near_copy(unit):
        return copy(part.at[unit, ways[unit][1]], near.at[unit], 3 * unit + 1, at_x(ways[unit][1]))

    def after_copy(unit):
        onward = ways[unit][0]
        return copy(part.at[unit, onward], after.at[unit], 3 * unit + 2, at_x(onward))

    def begin(each):
        each.start()
        sent.append(each)

    def relay(unit):
        far_copy(unit).wait_recv()
        part[unit, ways[unit][0]] += far[unit]
        begin(after_copy(unit))

    def y_copy(unit, other, slot):
        return pltpu.make_async_remote_copy(
            src_ref=part.at[unit, x, other // 4, lax.rem(other, 4)], dst_ref=line.at[unit, slot],
            send_sem=send_y.at[unit, other], recv_sem=recv_y.at[unit, slot],
            device_id=at_y(other), device_id_type=MESH,
        )

    def y_begin(unit):
        near_copy(unit).wait_recv()
        after_copy(unit).wait_recv()
        total = part[unit, x] + near[unit] + after[unit]
        if unit == 4:
            far_copy(unit).wait_recv()
            total = total + far[unit]
        part[unit, x] = total

        for step in (4, 3, 5, 2, 6, 1, 7):
            y_copy(unit, lax.rem(y + step, 8), y).start()

        line[unit, y] = part[unit, x, y_hi, y_lo]

    row = lax.rem(lax.broadcasted_iota(jnp.int32, (48, 256), 0), 24)
    lane = lax.broadcasted_iota(jnp.int32, (48, 256), 1)
    side, lane = lane // 128, lax.rem(lane, 128)
    rank = lax.rem(lane, 12)
    wanted = jnp.where(rank < 8, 8 * side + rank, 8 + 4 * side + rank)
    pick = ((row == wanted) & (lane < 120)).astype(f32).astype(bf16)
    lane_place = lax.broadcasted_iota(jnp.int32, (16, 256), 1)
    lane_place = lax.rem(lane_place, 128) // 12

    def y_end(unit):
        @pl.loop(1, 8)
        def _(step):
            other = lax.rem(y + step, 8)
            y_copy(unit, other, other).wait_recv()

        value = jnp.concatenate([jnp.sum(line[unit, 0:4], axis=0), jnp.sum(line[unit, 4:8], axis=0)], axis=1)
        turned = dot(jnp.concatenate(halves(value), axis=0), pick, TN)
        return turned.reshape(2, 8, 16, 256)

    def tile_rows(half, row):
        return pl.ds(8 * half + row, 16, stride=16)

    def unit_end(unit):
        turned = y_end(unit)
        for half in range(2):
            total = jnp.zeros((16, 256), f32)
            for place in range(8):
                total = jnp.where(lane_place == place, turned[half, place], total)
            for row in range(2):
                tiles[tile_rows(half, 2 * unit + row), :] = total[:, 128 * row : 128 * row + 128]

    def rest_end():
        turned = y_end(4)
        for half in range(2):
            for pair in range(4):
                total = jnp.where(lane_place == 8, turned[half, 2 * pair], turned[half, 2 * pair + 1])
                for row in range(2):
                    rows = tile_rows(half, 2 * pair + row)
                    lanes = slice(128 * row, 128 * row + 128)
                    tiles[rows, :] = jnp.where(lane_place[:, lanes] < 8, tiles[rows, :], total[:, lanes])

    columns(0)
    pl.semaphore_wait(barrier, 25)
    begin(far_copy(0))
    begin(near_copy(0))
    columns(1)
    begin(far_copy(1))
    begin(near_copy(1))
    columns(2)
    begin(near_copy(2))
    columns(3)
    frames(4, rest_hi[...].reshape(256, 256), rest_lo[...].reshape(256, 256))

    index_k = lax.broadcasted_iota(jnp.int32, (8, 1024), 0)
    index_l = lax.broadcasted_iota(jnp.int32, (8, 1024), 1) // 128
    spread = (index_k == index_l).astype(f32)

    for each in ("second_rows", "third_rows", "second_frames", "first_frames"):
        loads[each].wait()

    def widen(values):
        return lax.dot_general(values, spread, TN, precision=lax.Precision.HIGHEST, preferred_element_type=f32)

    wide_second = widen(second_rows[...])
    for row in range(8):
        lanes = slice(row * 128, row * 128 + 128)
        value = second_frames[...] * wide_second[:, lanes]
        hi, lo = halves(value)
        second_hi[0:128, lanes], second_lo[0:128, lanes] = hi[0:128], lo[0:128]
        for copies in range(4):
            rows = slice(128 + 32 * copies, 160 + 32 * copies)
            second_hi[rows, lanes], second_lo[rows, lanes] = hi[128:160], lo[128:160]
    third_wide[...] = widen(third_rows[...])

    second = (
        dot(split[:, 0:1024], second_hi[...], NT)
        + dot(split[:, 1024:2048], second_hi[...], NT)
        + dot(split[:, 0:1024], second_lo[...], NT)
    )
    main = second[:, 0:128].reshape(2, 8, 2, 16, 128)
    tail = second[:, 128:256].reshape(2, 8, 2, 2, 8, 128)
    quarter = lax.broadcasted_iota(jnp.int32, (8, 8, 128), 2) // 32
    for which in range(2):
        small[which, :, 0:16, :] = main[0, :, which]
        small[which, :, 16:32, :] = main[1, :, which]
        small[which, :, 32:40, :] = jnp.where(
            quarter < 2,
            jnp.where(quarter == 0, tail[0, :, which, 0], tail[0, :, which, 1]),
            jnp.where(quarter == 2, tail[1, :, which, 0], tail[1, :, which, 1]),
        )

    total = jnp.zeros((96, 128), f32)
    for row in range(8):
        place = slice((row % 2) * 128, (row % 2) * 128 + 128)
        total = total + inner[row // 2, 160:256, place] * third_wide[:, row * 128 : row * 128 + 128]
    frame_part[...] = total.reshape(2, 48, 128)

    other_core = (y_hi * 16 + z * 2 + 1 - core, tm)
    swap = copy(small.at[1 - core], core_in, 15, other_core)
    swap.start()
    swap_frames = copy(frame_part.at[1 - core], frame_in, 16, other_core)
    swap_frames.start()
    sent.extend([swap, swap_frames])

    relay(0)
    begin(far_copy(2))
    relay(1)
    begin(far_copy(3))

    rows_total = jnp.zeros((16, 160), f32)
    index_k = lax.broadcasted_iota(jnp.int32, (16, 256), 0)
    index_l = lax.broadcasted_iota(jnp.int32, (16, 256), 1) // 128
    for pair in range(4):
        value = inner[pair, 0:160, :] * jnp.concatenate([first_frames[...], first_frames[...]], axis=1)
        hi, lo = halves(value)
        ones = (index_k == index_l + 2 * pair).astype(f32).astype(bf16)
        rows_total = rows_total + dot(ones, hi, NT) + dot(ones, lo, NT)

    begin(near_copy(3))

    swap.wait_recv()
    layer_out[...] = small[core] + core_in[...]
    swap_frames.wait_recv()
    frame_layer[z] = frame_part[core] + frame_in[...]

    def layer_copy(other, slot, kind):
        if kind == 0:
            source, target = layer_out.at[other], layer_in.at[slot]
        else:
            source, target = frame_layer.at[z], frame_layer.at[slot]
        return pltpu.make_async_remote_copy(
            src_ref=source, dst_ref=target, send_sem=send_layer.at[kind, other], recv_sem=recv_layer.at[kind, slot],
            device_id=at_z(other), device_id_type=MESH,
        )

    @pl.loop(1, 8)
    def _(step):
        other = lax.rem(z + step, 8)
        layer_copy(other, z, 0).start()
        layer_copy(other, z, 1).start()

    layer_in[z] = layer_out[z]

    y_begin(0)
    relay(2)
    begin(near_copy(4))
    begin(after_copy(4))
    y_begin(1)
    relay(3)
    begin(far_copy(4))
    y_begin(2)

    @pl.loop(1, 8)
    def _(step):
        other = lax.rem(z + step, 8)
        layer_copy(other, other, 0).wait_recv()
        layer_copy(other, other, 1).wait_recv()

    line_out[0:40, :] = jnp.sum(layer_in[...], axis=0)
    line_out[40:48, :] = rows_total[0:8, 0:128]
    line_out[48:56, :] = jnp.concatenate([rows_total[0:8, 128:160], jnp.zeros((8, 96), f32)], axis=1)
    frame_other[...] = jnp.sum(frame_layer[...], axis=0)

    def line_copy(other, slot):
        return pltpu.make_async_remote_copy(
            src_ref=line_out, dst_ref=line_in.at[slot], send_sem=send_line.at[other], recv_sem=recv_line.at[slot],
            device_id=at_x(other), device_id_type=MESH,
        )

    for step in (1, 2, 3):
        line_copy(lax.rem(x + step, 4), x).start()
    line_in[x] = line_out[...]
    flip = copy(frame_other, frame_last, 17, (lax.rem(space + 16, 32), tm))
    flip.start()
    sent.append(flip)

    y_begin(3)
    unit_end(0)
    y_begin(4)
    unit_end(1)

    for step in (1, 2, 3):
        other = lax.rem(x + step, 4)
        line_copy(other, other).wait_recv()
    summed = jnp.sum(line_in[...], axis=0)
    for half in range(2):
        ring_out[half, 0:16, :] = summed[16 * half : 16 * half + 16]
        ring_out[half, 16:40, :] = summed[32:56]

    def ring_copy(other, slot):
        return pltpu.make_async_remote_copy(
            src_ref=ring_out.at[other // 4], dst_ref=ring_in.at[slot], send_sem=send_ring.at[other], recv_sem=recv_ring.at[slot],
            device_id=at_y(other), device_id_type=MESH,
        )

    @pl.loop(1, 8)
    def _(step):
        ring_copy(lax.rem(y + step, 8), y).start()

    ring_in[y] = ring_out[y_hi]

    flip.wait_recv()
    frame_in_place = frame_other[...] + frame_last[...]
    out_frames[core] = frame_in_place
    swap_back = copy(out_frames.at[core], out_frames.at[core], 18, other_core)
    swap_back.start()
    sent.append(swap_back)

    unit_end(2)
    unit_end(3)
    rest_end()

    mine = lax.rem(space, 16)
    tile_view = tiles.reshape(16, 2, 8, 128)

    def tile_copy(other, slot):
        return pltpu.make_async_remote_copy(
            src_ref=tile_view.at[other], dst_ref=gathered.at[:, slot],
            send_sem=send_space.at[other], recv_sem=recv_space.at[slot],
            device_id=(y_hi * 16 + other, tm), device_id_type=MESH,
        )

    for step in (8, 7, 9, 6, 10, 5, 11, 4, 12, 3, 13, 2, 14, 1, 15):
        tile_copy(lax.rem(mine + step, 16), mine).start()

    gathered[:, mine] = tile_view[mine]

    @pl.loop(1, 8)
    def _(step):
        other = lax.rem(y + step, 8)
        ring_copy(other, other).wait_recv()

    final = jnp.sum(ring_in[:, 0:24, :], axis=0)
    out_small[0:24, :] = final
    out_small[24:40, :] = jnp.sum(ring_in[pl.ds(y_hi * 4, 4), 24:40, :], axis=0)

    @pl.when(y_hi == 0)
    def _():
        out_small[16:24, 0:64] = final[16:24, 0:64]

    @pl.when(y_hi == 1)
    def _():
        out_small[16:24, 0:64] = final[16:24, 64:128]

    for each in sent:
        each.wait_send()

    @pl.loop(1, 8)
    def _(step):
        other = lax.rem(z + step, 8)
        layer_copy(other, z, 0).wait_send()
        layer_copy(other, z, 1).wait_send()
        other = lax.rem(y + step, 8)
        ring_copy(other, y).wait_send()
        for unit in range(5):
            y_copy(unit, other, y).wait_send()

    for step in (1, 2, 3):
        line_copy(lax.rem(x + step, 4), x).wait_send()

    @pl.loop(1, 16)
    def _(step):
        tile_copy(lax.rem(mine + step, 16), mine).wait_send()

    @pl.loop(1, 16)
    def _(step):
        other = lax.rem(mine + step, 16)
        tile_copy(other, other).wait_recv()

    swap_back.wait_recv()


def finish(gathered, small, frames, core_rows, out_rows, out_cols, out_frames, out_core):
    out_rows[:, 0:128] = small[24:32, :]
    out_rows[:, 128:160] = small[32:40, 0:32]
    out_cols[:, 0:128] = small[0:16, :]
    for half in range(2):
        out_cols[8 * half : 8 * half + 8, 128:160] = small[16:24, 32 * half : 32 * half + 32]
    out_frames[...] = frames[...]
    hi, lo = halves(gathered[...].reshape(256, 128).T)
    rows_hi, rows_lo = halves(core_rows[...])
    result = dot(hi, rows_hi, NT) + dot(hi, rows_lo, NT) + dot(lo, rows_hi, NT)
    for place in range(10):
        out_core[place] = result[12 * place : 12 * place + 12]


def per_device(
    video_slab, first_cols, first_frames, second_rows, second_frames, third_rows, third_cols, core_rows, core_cols, core_frames,
):
    arguments = (
        video_slab, first_cols.T, third_cols.T, core_cols.T, first_frames.T, second_frames.T, core_frames.T,
        second_rows, third_rows,
    )
    vmem = pl.BlockSpec(memory_space=pltpu.VMEM)
    dma = pltpu.SemaphoreType.DMA
    scratch = [pltpu.VMEM(each.shape, f32) for each in arguments] + [
        pltpu.VMEM((4, 320, 128), f32),
        pltpu.VMEM((576, 512), bf16), pltpu.VMEM((576, 512), bf16),
        pltpu.VMEM((384, 256), bf16), pltpu.VMEM((384, 256), bf16),
        pltpu.VMEM((512, 2048), bf16),
        pltpu.VMEM((4, 256, 256), f32),
        pltpu.VMEM((2, 4, 32, 256), bf16), pltpu.VMEM((2, 4, 32, 256), bf16),
        pltpu.VMEM((256, 1024), bf16), pltpu.VMEM((256, 1024), bf16),
        pltpu.VMEM((96, 1024), f32),
        pltpu.VMEM((5, 4, 2, 4, 24, 128), f32), *[pltpu.VMEM((5, 2, 4, 24, 128), f32)] * 3,
        pltpu.VMEM((5, 8, 24, 128), f32),
        pltpu.VMEM((256, 128), f32),
        pltpu.VMEM((2, 8, 40, 128), f32), pltpu.VMEM((8, 40, 128), f32),
        pltpu.VMEM((8, 40, 128), f32), pltpu.VMEM((8, 40, 128), f32),
        pltpu.VMEM((2, 48, 128), f32), pltpu.VMEM((48, 128), f32), pltpu.VMEM((8, 48, 128), f32),
        pltpu.VMEM((48, 128), f32), pltpu.VMEM((48, 128), f32),
        pltpu.VMEM((56, 128), f32), pltpu.VMEM((4, 56, 128), f32),
        pltpu.VMEM((2, 40, 128), f32), pltpu.VMEM((8, 40, 128), f32),
        dma((12,)), dma((20,)), dma((20,)), dma((16,)), dma((16,)), dma((2, 8)), dma((2, 8)), dma((4,)), dma((4,)), dma((8,)), dma((8,)), dma((5, 8)), dma((5, 8)),
    ]
    gathered, small, frames = pl.pallas_call(
        kernel,
        out_shape=[
            jax.ShapeDtypeStruct((2, 16, 8, 128), f32),
            jax.ShapeDtypeStruct((40, 128), f32),
            jax.ShapeDtypeStruct((2, 48, 128), f32),
        ],
        in_specs=[pl.BlockSpec(memory_space=pltpu.HBM)] * 9,
        out_specs=[vmem] * 3,
        scratch_shapes=scratch,
        compiler_params=pltpu.CompilerParams(collective_id=0, has_side_effects=True, vmem_limit_bytes=60 * 2**20),
    )(*arguments)
    rows, cols, frames, core = pl.pallas_call(
        finish,
        out_shape=[
            jax.ShapeDtypeStruct((8, 160), f32),
            jax.ShapeDtypeStruct((16, 160), f32),
            jax.ShapeDtypeStruct((2, 48, 128), f32),
            jax.ShapeDtypeStruct((10, 12, 320), f32),
        ],
        in_specs=[vmem] * 4,
        out_specs=[vmem] * 4,
        compiler_params=pltpu.CompilerParams(vmem_limit_bytes=60 * 2**20),
    )(gathered, small, frames, core_rows.T)
    return rows, cols, frames.reshape(96, 128).T, core.transpose(2, 0, 1)


def solution(mesh):
    return jax.shard_map(
        per_device,
        mesh=mesh,
        in_specs=(
            P("space", None, "tm"),
            P(),
            P("tm", None),
            P("space", None),
            P("tm", None),
            P("space", None),
            P(),
            P(),
            P(),
            P("tm", None),
        ),
        out_specs=(P("space", None), P("space", None), P("tm", None), P(None, "space", "tm")),
        check_vma=False,
    )
```

```python
import functools

import jax
import jax.numpy as jnp
from jax import lax
from jax.experimental import pallas as pl
from jax.experimental.pallas import tpu as pltpu
from jax.sharding import PartitionSpec as P

MESH = pl.DeviceIdType.MESH
f32, bf16 = jnp.float32, jnp.bfloat16

NN = (((1,), (0,)), ((), ()))
NT = (((1,), (1,)), ((), ()))
TN = (((0,), (0,)), ((), ()))


def dot(a, b, dims=NN):
    return lax.dot_general(a, b, dims, preferred_element_type=f32)


def halves(a):
    high = a.astype(bf16)
    return high, (a - high.astype(f32)).astype(bf16)


def kernel(
    slab_given, first_cols_given, third_cols_given, core_cols_given, first_frames_given, second_frames_given,
    core_frames_given, second_rows_given, third_rows_given,
    gathered, out_small, out_frames,
    slab, first_cols, third_cols, core_cols, first_frames, second_frames, core_frames, second_rows, third_rows,
    order, cols_hi, cols_lo, frames_hi, frames_lo, split, inner, rest_hi, rest_lo, second_hi, second_lo, third_wide,
    part, far, near, after, line, tiles,
    small, core_in, layer_out, layer_in, frame_part, frame_in, frame_pair, frame_other, frame_layer,
    line_out, line_in, ring_in, piece_in,
    load_sem, send_sem, recv_sem, send_space, recv_space, send_layer, recv_layer, send_line, recv_line, send_ring, recv_ring, send_y, recv_y,
    send_piece, recv_piece, send_quarter, recv_quarter,
):
    space, tm = lax.axis_index("space"), lax.axis_index("tm")
    y_hi, z, core = space // 16, lax.rem(space // 2, 8), lax.rem(space, 2)
    y_lo, x = tm // 4, lax.rem(tm, 4)
    y = y_hi * 4 + y_lo

    def at_x(other):
        return (space, y_lo * 4 + other)

    def at_y(other):
        return (lax.rem(other // 4, 2) * 16 + z * 2 + core, lax.rem(other, 4) * 4 + x)

    def at_z(other):
        return (y_hi * 16 + other * 2 + core, tm)

    def load(number, source, target):
        return pltpu.make_async_copy(source, target, load_sem.at[number])

    def load_pair(pair):
        rows = pl.ds(2 * pair, 2)
        return load(pair, slab_given.at[rows], slab.at[rows])

    loads = {
        "core_cols": load(4, core_cols_given, core_cols),
        "first_cols": load(5, first_cols_given, first_cols),
        "third_cols": load(6, third_cols_given, third_cols),
        "core_frames": load(7, core_frames_given, core_frames),
        "second_rows": load(8, second_rows_given, second_rows),
        "third_rows": load(9, third_rows_given, third_rows),
        "second_frames": load(10, second_frames_given, second_frames),
        "first_frames": load(11, first_frames_given, first_frames),
    }
    loads["core_cols"].start()
    load_pair(0).start()
    loads["core_frames"].start()
    for pair in (1, 2, 3):
        load_pair(pair).start()
    for each in ("first_cols", "third_cols", "second_rows", "third_rows", "second_frames", "first_frames"):
        loads[each].start()

    barrier = pltpu.get_barrier_semaphore()

    def greet(device):
        pl.semaphore_signal(barrier, inc=1, device_id=device, device_id_type=MESH)

    @pl.loop(1, 16)
    def _(step):
        greet((y_hi * 16 + lax.rem(space + step, 16), tm))

    @pl.loop(1, 8)
    def _(step):
        greet(at_y(lax.rem(y + step, 8)))

    greet(((1 - y_hi) * 16 + z * 2 + 1 - core, tm))
    for step in (1, 2, 3):
        greet(at_x(lax.rem(x + step, 4)))

    loads["core_cols"].wait()

    for quarter in range(4):
        lanes = slice(128 * quarter, 128 * quarter + 128)
        order[quarter] = core_cols[:, lanes]
        for half in range(2):
            for place in range(10):
                hi, lo = halves(order[quarter, pl.ds(160 * half + place, 16, stride=10), :])
                base = 256 + 128 * half + 16 * place if place < 8 else 512 + 32 * half + 16 * (place - 8)
                cols_hi[base : base + 16, lanes], cols_lo[base : base + 16, lanes] = hi, lo

    loads["core_frames"].wait()

    for other in range(4):
        for place in range(4):
            base = 12 * (place * 4 + other)
            row = 24 * (other * 4 + place)
            eight = core_frames[base : base + 8, :]
            four = core_frames[base + 8 : base + 12, :]
            blank = jnp.zeros((8, 128), f32)
            blank4 = jnp.zeros((4, 128), f32)
            block = jnp.concatenate(
                [
                    jnp.concatenate([eight, blank], axis=1),
                    jnp.concatenate([blank, eight], axis=1),
                    jnp.concatenate([four, blank4], axis=1),
                    jnp.concatenate([blank4, four], axis=1),
                ],
                axis=0,
            )
            hi, lo = halves(block)
            frames_hi[row : row + 24, :], frames_lo[row : row + 24, :] = hi, lo

    def columns(pair):
        load_pair(pair).wait()
        block = jnp.concatenate([slab[2 * pair], slab[2 * pair + 1]], axis=1)
        hi, lo = halves(block)
        split[:, pair * 256 : pair * 256 + 256] = hi
        split[:, pair * 256 + 1024 : pair * 256 + 1280] = lo
        product = dot(cols_hi[256:576], hi) + dot(cols_hi[256:576], lo) + dot(cols_lo[256:576], hi)
        hi, lo = halves(product[256:320, :].reshape(2, 32, 256))
        rest_hi[:, pair], rest_lo[:, pair] = hi, lo
        frames(pair, *halves(product[0:256, :]))

    def other_columns(pair):
        hi = split[:, pair * 256 : pair * 256 + 256]
        lo = split[:, pair * 256 + 1024 : pair * 256 + 1280]
        inner[pair] = dot(cols_hi[0:256], hi) + dot(cols_hi[0:256], lo) + dot(cols_lo[0:256], hi)

    def frames(unit, right_hi, right_lo):
        product = (
            dot(frames_hi[...], right_hi, NT) + dot(frames_hi[...], right_lo, NT) + dot(frames_lo[...], right_hi, NT)
        )
        for half in range(2):
            part[unit, :, half] = product[:, 128 * half : 128 * half + 128].reshape(4, 4, 24, 128)

    def copy(source, target, number, device):
        return pltpu.make_async_remote_copy(
            src_ref=source, dst_ref=target, send_sem=send_sem.at[number], recv_sem=recv_sem.at[number],
            device_id=device, device_id_type=MESH,
        )

    right, left, across = lax.rem(x + 1, 4), lax.rem(x + 3, 4), lax.rem(x + 2, 4)

    sent = []

    ways = ((right, left), (left, right), (right, left), (left, right), (right, left), (left, right))

    def own(piece, owner):
        return part.at[piece, owner] if piece < 4 else part.at[4, owner, piece - 4]

    def landing(ref, piece):
        return ref.at[piece] if piece < 4 else ref.at[4, piece - 4]

    def far_copy(piece):
        return copy(own(piece, across), landing(far, piece), 3 * piece, at_x(ways[piece][0]))

    def near_copy(piece):
        back = ways[piece][1]
        return copy(own(piece, back), landing(near, piece), 3 * piece + 1, at_x(back))

    def after_copy(piece):
        onward = ways[piece][0]
        return copy(own(piece, onward), landing(after, piece), 3 * piece + 2, at_x(onward))

    def begin(each):
        each.start()
        sent.append(each)

    def relay(piece):
        far_copy(piece).wait_recv()
        if piece < 4:
            part[piece, ways[piece][0]] += far[piece]
        else:
            part[4, ways[piece][0], piece - 4] += far[4, piece - 4]
        begin(after_copy(piece))

    def y_copy(unit, other, slot):
        return pltpu.make_async_remote_copy(
            src_ref=part.at[unit, x, other // 4, lax.rem(other, 4)], dst_ref=line.at[unit, slot],
            send_sem=send_y.at[unit, other], recv_sem=recv_y.at[unit, slot],
            device_id=at_y(other), device_id_type=MESH,
        )

    def y_begin(unit):
        for piece in (unit,) if unit < 4 else (4, 5):
            near_copy(piece).wait_recv()
            after_copy(piece).wait_recv()
        part[unit, x] = part[unit, x] + near[unit] + after[unit]

        for step in (4, 3, 5, 2, 6, 1, 7):
            y_copy(unit, lax.rem(y + step, 8), y).start()

        line[unit, y] = part[unit, x, y_hi, y_lo]

    row = lax.rem(lax.broadcasted_iota(jnp.int32, (48, 256), 0), 24)
    lane = lax.broadcasted_iota(jnp.int32, (48, 256), 1)
    side, lane = lane // 128, lax.rem(lane, 128)
    rank = lax.rem(lane, 12)
    wanted = jnp.where(rank < 8, 8 * side + rank, 8 + 4 * side + rank)
    pick = ((row == wanted) & (lane < 120)).astype(f32).astype(bf16)
    lane_place = lax.broadcasted_iota(jnp.int32, (16, 256), 1)
    lane_place = lax.rem(lane_place, 128) // 12

    def y_end(unit):
        @pl.loop(1, 8)
        def _(step):
            other = lax.rem(y + step, 8)
            y_copy(unit, other, other).wait_recv()

        value = jnp.concatenate([jnp.sum(line[unit, 0:4], axis=0), jnp.sum(line[unit, 4:8], axis=0)], axis=1)
        turned = dot(jnp.concatenate(halves(value), axis=0), pick, TN)
        return turned.reshape(2, 8, 16, 256)

    def tile_rows(half, row):
        return pl.ds(8 * half + row, 16, stride=16)

    def unit_end(unit):
        turned = y_end(unit)
        for half in range(2):
            total = jnp.zeros((16, 256), f32)
            for place in range(8):
                total = jnp.where(lane_place == place, turned[half, place], total)
            for row in range(2):
                tiles[tile_rows(half, 2 * unit + row), :] = total[:, 128 * row : 128 * row + 128]

    def rest_end():
        turned = y_end(4)
        for half in range(2):
            for pair in range(4):
                total = jnp.where(lane_place == 8, turned[half, 2 * pair], turned[half, 2 * pair + 1])
                for row in range(2):
                    rows = tile_rows(half, 2 * pair + row)
                    lanes = slice(128 * row, 128 * row + 128)
                    tiles[rows, :] = jnp.where(lane_place[:, lanes] < 8, tiles[rows, :], total[:, lanes])

    columns(0)
    pl.semaphore_wait(barrier, 26)
    begin(far_copy(0))
    begin(near_copy(0))
    columns(1)
    begin(far_copy(1))
    begin(near_copy(1))
    columns(2)
    begin(far_copy(2))
    columns(3)
    begin(far_copy(3))
    frames(4, rest_hi[...].reshape(256, 256), rest_lo[...].reshape(256, 256))

    loads["first_cols"].wait()
    loads["third_cols"].wait()
    hi, lo = halves(first_cols[...])
    cols_hi[0:160, :], cols_lo[0:160, :] = hi, lo
    hi, lo = halves(third_cols[...])
    cols_hi[160:256, :], cols_lo[160:256, :] = hi, lo
    for pair in range(4):
        other_columns(pair)

    relay(0)
    begin(far_copy(4))
    begin(near_copy(2))

    index_k = lax.broadcasted_iota(jnp.int32, (8, 1024), 0)
    index_l = lax.broadcasted_iota(jnp.int32, (8, 1024), 1) // 128
    spread = (index_k == index_l).astype(f32)

    for each in ("second_rows", "third_rows", "second_frames", "first_frames"):
        loads[each].wait()

    def widen(values):
        return lax.dot_general(values, spread, TN, precision=lax.Precision.HIGHEST, preferred_element_type=f32)

    wide_second = widen(second_rows[...])
    for row in range(8):
        lanes = slice(row * 128, row * 128 + 128)
        value = second_frames[...] * wide_second[:, lanes]
        hi, lo = halves(value)
        second_hi[0:128, lanes], second_lo[0:128, lanes] = hi[0:128], lo[0:128]
        for copies in range(4):
            rows = slice(128 + 32 * copies, 160 + 32 * copies)
            second_hi[rows, lanes], second_lo[rows, lanes] = hi[128:160], lo[128:160]
    third_wide[...] = widen(third_rows[...])

    second = (
        dot(split[:, 0:1024], second_hi[...], NT)
        + dot(split[:, 1024:2048], second_hi[...], NT)
        + dot(split[:, 0:1024], second_lo[...], NT)
    )
    main = second[:, 0:128].reshape(2, 8, 2, 16, 128)
    tail = second[:, 128:256].reshape(2, 8, 2, 2, 8, 128)
    quarter = lax.broadcasted_iota(jnp.int32, (8, 8, 128), 2) // 32
    for which in range(2):
        small[which, :, 0:16, :] = main[0, :, which]
        small[which, :, 16:32, :] = main[1, :, which]
        small[which, :, 32:40, :] = jnp.where(
            quarter < 2,
            jnp.where(quarter == 0, tail[0, :, which, 0], tail[0, :, which, 1]),
            jnp.where(quarter == 2, tail[1, :, which, 0], tail[1, :, which, 1]),
        )

    relay(1)
    begin(far_copy(5))

    total = jnp.zeros((96, 128), f32)
    for row in range(8):
        place = slice((row % 2) * 128, (row % 2) * 128 + 128)
        total = total + inner[row // 2, 160:256, place] * third_wide[:, row * 128 : row * 128 + 128]
    frame_part[...] = total.reshape(2, 2, 24, 128)

    other_core = (y_hi * 16 + z * 2 + 1 - core, tm)
    swap = copy(small.at[1 - core], core_in, 18, other_core)
    swap.start()
    swap_frames = copy(frame_part.at[1 - core], frame_in, 19, other_core)
    swap_frames.start()
    sent.extend([swap, swap_frames])

    relay(2)
    begin(near_copy(3))

    swap.wait_recv()
    layer_out[...] = small[core] + core_in[...]
    swap_frames.wait_recv()
    frame_pair[...] = frame_part[core] + frame_in[...]

    def layer_copy(other, slot):
        return pltpu.make_async_remote_copy(
            src_ref=layer_out.at[other], dst_ref=layer_in.at[slot], send_sem=send_layer.at[0, other],
            recv_sem=recv_layer.at[0, slot], device_id=at_z(other), device_id_type=MESH,
        )

    def frame_copy(other, slot):
        return pltpu.make_async_remote_copy(
            src_ref=frame_layer.at[z], dst_ref=frame_layer.at[slot], send_sem=send_layer.at[1, other],
            recv_sem=recv_layer.at[1, slot], device_id=at_z(other), device_id_type=MESH,
        )

    for step in (4, 3, 5, 2, 6, 1, 7):
        layer_copy(lax.rem(z + step, 8), z).start()
    layer_in[z] = layer_out[z]
    flip = copy(frame_pair.at[1 - y_hi], frame_other, 20, (lax.rem(space + 16, 32), tm))
    begin(flip)

    relay(3)
    y_begin(0)

    rows_total = jnp.zeros((16, 160), f32)
    index_k = lax.broadcasted_iota(jnp.int32, (16, 256), 0)
    index_l = lax.broadcasted_iota(jnp.int32, (16, 256), 1) // 128
    for pair in range(4):
        value = inner[pair, 0:160, :] * jnp.concatenate([first_frames[...], first_frames[...]], axis=1)
        hi, lo = halves(value)
        ones = (index_k == index_l + 2 * pair).astype(f32).astype(bf16)
        rows_total = rows_total + dot(ones, hi, NT) + dot(ones, lo, NT)

    y_begin(1)
    relay(4)
    begin(near_copy(5))
    begin(near_copy(4))
    relay(5)
    y_begin(2)
    unit_end(0)
    y_begin(3)

    flip.wait_recv()
    frame_layer[z] = frame_pair[y_hi] + frame_other[...]
    for step in (4, 3, 5, 2, 6, 1, 7):
        frame_copy(lax.rem(z + step, 8), z).start()

    @pl.loop(1, 8)
    def _(step):
        other = lax.rem(z + step, 8)
        layer_copy(other, other).wait_recv()

    line_out[0:40, :] = jnp.sum(layer_in[...], axis=0)
    line_out[40:48, :] = jnp.zeros((8, 128), f32)
    line_out[48:56, :] = rows_total[0:8, 0:128]
    line_out[56:64, :] = jnp.concatenate([rows_total[0:8, 128:160], jnp.zeros((8, 96), f32)], axis=1)

    def line_copy(other, slot):
        return pltpu.make_async_remote_copy(
            src_ref=line_out.at[pl.ds(pl.multiple_of(other * 16, 16), 16)], dst_ref=line_in.at[slot],
            send_sem=send_line.at[other], recv_sem=recv_line.at[slot],
            device_id=at_x(other), device_id_type=MESH,
        )

    for step in (2, 1, 3):
        line_copy(lax.rem(x + step, 4), x).start()
    line_in[x] = line_out[pl.ds(pl.multiple_of(x * 16, 16), 16)]

    y_begin(4)
    unit_end(1)
    unit_end(2)

    for step in (1, 2, 3):
        other = lax.rem(x + step, 4)
        line_copy(other, other).wait_recv()
    ring_in[y] = jnp.sum(line_in[...], axis=0)

    def ring_copy(other, slot):
        return pltpu.make_async_remote_copy(
            src_ref=ring_in.at[y], dst_ref=ring_in.at[slot], send_sem=send_ring.at[other], recv_sem=recv_ring.at[slot],
            device_id=at_y(other), device_id_type=MESH,
        )

    for step in (4, 3, 5, 2, 6, 1, 7):
        ring_copy(lax.rem(y + step, 8), y).start()

    unit_end(3)

    @pl.loop(1, 8)
    def _(step):
        other = lax.rem(z + step, 8)
        frame_copy(other, other).wait_recv()

    out_frames[core, y_hi] = jnp.sum(frame_layer[...], axis=0)

    def quarter_copy(device_core, device_half, slot_core, slot_half):
        return pltpu.make_async_remote_copy(
            src_ref=out_frames.at[core, y_hi], dst_ref=out_frames.at[slot_core, slot_half],
            send_sem=send_quarter.at[device_core, device_half], recv_sem=recv_quarter.at[slot_core, slot_half],
            device_id=(device_half * 16 + z * 2 + device_core, tm), device_id_type=MESH,
        )

    others = ((core, 1 - y_hi), (1 - core, 1 - y_hi), (1 - core, y_hi))
    for other in others:
        begin(quarter_copy(*other, core, y_hi))

    rest_end()

    mine = lax.rem(space, 16)
    tile_view = tiles.reshape(16, 2, 8, 128)

    def tile_copy(other, slot):
        return pltpu.make_async_remote_copy(
            src_ref=tile_view.at[other], dst_ref=gathered.at[:, slot],
            send_sem=send_space.at[other], recv_sem=recv_space.at[slot],
            device_id=(y_hi * 16 + other, tm), device_id_type=MESH,
        )

    for step in (8, 7, 9, 6, 10, 5, 11, 4, 12, 3, 13, 2, 14, 1, 15):
        tile_copy(lax.rem(mine + step, 16), mine).start()

    gathered[:, mine] = tile_view[mine]

    @pl.loop(1, 8)
    def _(step):
        other = lax.rem(y + step, 8)
        ring_copy(other, other).wait_recv()

    half_sum = jnp.sum(ring_in[pl.ds(y_hi * 4, 4)], axis=0)
    piece_in[x] = jnp.where(x == 3, half_sum, jnp.sum(ring_in[...], axis=0))

    def piece_copy(other, slot):
        return pltpu.make_async_remote_copy(
            src_ref=piece_in.at[x], dst_ref=piece_in.at[slot], send_sem=send_piece.at[other], recv_sem=recv_piece.at[slot],
            device_id=at_x(other), device_id_type=MESH,
        )

    for step in (2, 1, 3):
        piece_copy(lax.rem(x + step, 4), x).start()

    for each in sent:
        each.wait_send()

    @pl.loop(1, 8)
    def _(step):
        other = lax.rem(z + step, 8)
        layer_copy(other, z).wait_send()
        frame_copy(other, z).wait_send()
        other = lax.rem(y + step, 8)
        ring_copy(other, y).wait_send()
        for unit in range(5):
            y_copy(unit, other, y).wait_send()

    for step in (1, 2, 3):
        other = lax.rem(x + step, 4)
        line_copy(other, x).wait_send()
        piece_copy(other, x).wait_send()

    @pl.loop(1, 16)
    def _(step):
        tile_copy(lax.rem(mine + step, 16), mine).wait_send()

    for step in (1, 2, 3):
        other = lax.rem(x + step, 4)
        piece_copy(other, other).wait_recv()
    out_small[0:16, :] = piece_in[y_hi]
    out_small[16:24, :] = piece_in[2, 0:8]

    @pl.when(y_hi == 1)
    def _():
        out_small[16:24, 0:64] = piece_in[2, 0:8, 64:128]

    out_small[24:40, :] = piece_in[3]
    for other in others:
        quarter_copy(*other, *other).wait_recv()

    @pl.loop(1, 16)
    def _(step):
        other = lax.rem(mine + step, 16)
        tile_copy(other, other).wait_recv()


def finish(gathered, small, frames, core_rows, out_rows, out_cols, out_frames, out_core):
    out_rows[:, 0:128] = small[24:32, :]
    out_rows[:, 128:160] = small[32:40, 0:32]
    out_cols[:, 0:128] = small[0:16, :]
    for half in range(2):
        out_cols[8 * half : 8 * half + 8, 128:160] = small[16:24, 32 * half : 32 * half + 32]
    out_frames[...] = frames[...]
    hi, lo = halves(gathered[...].reshape(256, 128).T)
    rows_hi, rows_lo = halves(core_rows[...])
    result = dot(hi, rows_hi, NT) + dot(hi, rows_lo, NT) + dot(lo, rows_hi, NT)
    for place in range(10):
        out_core[place] = result[12 * place : 12 * place + 12]


def per_device(
    video_slab, first_cols, first_frames, second_rows, second_frames, third_rows, third_cols, core_rows, core_cols, core_frames,
):
    arguments = (
        video_slab, first_cols.T, third_cols.T, core_cols.T, first_frames.T, second_frames.T, core_frames.T,
        second_rows, third_rows,
    )
    vmem = pl.BlockSpec(memory_space=pltpu.VMEM)
    dma = pltpu.SemaphoreType.DMA
    scratch = [pltpu.VMEM(each.shape, f32) for each in arguments] + [
        pltpu.VMEM((4, 320, 128), f32),
        pltpu.VMEM((576, 512), bf16), pltpu.VMEM((576, 512), bf16),
        pltpu.VMEM((384, 256), bf16), pltpu.VMEM((384, 256), bf16),
        pltpu.VMEM((512, 2048), bf16),
        pltpu.VMEM((4, 256, 256), f32),
        pltpu.VMEM((2, 4, 32, 256), bf16), pltpu.VMEM((2, 4, 32, 256), bf16),
        pltpu.VMEM((256, 1024), bf16), pltpu.VMEM((256, 1024), bf16),
        pltpu.VMEM((96, 1024), f32),
        pltpu.VMEM((5, 4, 2, 4, 24, 128), f32), *[pltpu.VMEM((5, 2, 4, 24, 128), f32)] * 3,
        pltpu.VMEM((5, 8, 24, 128), f32),
        pltpu.VMEM((256, 128), f32),
        pltpu.VMEM((2, 8, 40, 128), f32), pltpu.VMEM((8, 40, 128), f32),
        pltpu.VMEM((8, 40, 128), f32), pltpu.VMEM((8, 40, 128), f32),
        pltpu.VMEM((2, 2, 24, 128), f32), pltpu.VMEM((2, 24, 128), f32), pltpu.VMEM((2, 24, 128), f32),
        pltpu.VMEM((24, 128), f32), pltpu.VMEM((8, 24, 128), f32),
        pltpu.VMEM((64, 128), f32), pltpu.VMEM((4, 16, 128), f32), pltpu.VMEM((8, 16, 128), f32), pltpu.VMEM((4, 16, 128), f32),
        dma((12,)), dma((22,)), dma((22,)), dma((16,)), dma((16,)), dma((2, 8)), dma((2, 8)), dma((4,)), dma((4,)), dma((8,)), dma((8,)), dma((5, 8)), dma((5, 8)),
        dma((4,)), dma((4,)), dma((2, 2)), dma((2, 2)),
    ]
    gathered, small, frames = pl.pallas_call(
        kernel,
        out_shape=[
            jax.ShapeDtypeStruct((2, 16, 8, 128), f32),
            jax.ShapeDtypeStruct((40, 128), f32),
            jax.ShapeDtypeStruct((2, 2, 24, 128), f32),
        ],
        in_specs=[pl.BlockSpec(memory_space=pltpu.HBM)] * 9,
        out_specs=[vmem] * 3,
        scratch_shapes=scratch,
        compiler_params=pltpu.CompilerParams(collective_id=0, has_side_effects=True, vmem_limit_bytes=60 * 2**20),
    )(*arguments)
    rows, cols, frames, core = pl.pallas_call(
        finish,
        out_shape=[
            jax.ShapeDtypeStruct((8, 160), f32),
            jax.ShapeDtypeStruct((16, 160), f32),
            jax.ShapeDtypeStruct((2, 2, 24, 128), f32),
            jax.ShapeDtypeStruct((10, 12, 320), f32),
        ],
        in_specs=[vmem] * 4,
        out_specs=[vmem] * 4,
        compiler_params=pltpu.CompilerParams(vmem_limit_bytes=60 * 2**20),
    )(gathered, small, frames, core_rows.T)
    return rows, cols, frames.reshape(96, 128).T, core.transpose(2, 0, 1)


def solution(mesh):
    return jax.shard_map(
        per_device,
        mesh=mesh,
        in_specs=(
            P("space", None, "tm"),
            P(),
            P("tm", None),
            P("space", None),
            P("tm", None),
            P("space", None),
            P(),
            P(),
            P(),
            P("tm", None),
        ),
        out_specs=(P("space", None), P("space", None), P("tm", None), P(None, "space", "tm")),
        check_vma=False,
    )
```

```python
import functools

import jax
import jax.numpy as jnp
from jax import lax
from jax.experimental import pallas as pl
from jax.experimental.pallas import tpu as pltpu
from jax.sharding import PartitionSpec as P

MESH = pl.DeviceIdType.MESH
f32, bf16 = jnp.float32, jnp.bfloat16

NN = (((1,), (0,)), ((), ()))
NT = (((1,), (1,)), ((), ()))
TN = (((0,), (0,)), ((), ()))


def dot(a, b, dims=NN):
    return lax.dot_general(a, b, dims, preferred_element_type=f32)


def halves(a):
    high = a.astype(bf16)
    return high, (a - high.astype(f32)).astype(bf16)


def kernel(
    slab_given, first_cols_given, third_cols_given, core_cols_given, first_frames_given, second_frames_given,
    core_frames_given, second_rows_given, third_rows_given,
    gathered, out_small, out_frames,
    small_sums, frame_sums,
    slab, first_cols, third_cols, core_cols, first_frames, second_frames, core_frames, second_rows, third_rows,
    order, cols_hi, cols_lo, frames_hi, frames_lo, split, inner, rest_hi, rest_lo, second_hi, second_lo, third_wide,
    part, far, near, after, line, tiles,
    small, core_in, layer_out, layer_in, frame_part, frame_in, frame_pair, frame_other, frame_layer,
    line_out, line_in, ring_in, piece_in,
    load_sem, send_sem, recv_sem, send_space, recv_space, send_layer, recv_layer, send_line, recv_line, send_ring, recv_ring, send_y, recv_y,
    send_piece, recv_piece, send_quarter, recv_quarter,
):
    space, tm = lax.axis_index("space"), lax.axis_index("tm")
    y_hi, z, core = space // 16, lax.rem(space // 2, 8), lax.rem(space, 2)
    y_lo, x = tm // 4, lax.rem(tm, 4)
    y = y_hi * 4 + y_lo

    def at_x(other):
        return (space, y_lo * 4 + other)

    def at_y(other):
        return (lax.rem(other // 4, 2) * 16 + z * 2 + core, lax.rem(other, 4) * 4 + x)

    def at_z(other):
        return (y_hi * 16 + other * 2 + core, tm)

    def load(number, source, target):
        return pltpu.make_async_copy(source, target, load_sem.at[number])

    def load_pair(pair):
        rows = pl.ds(2 * pair, 2)
        return load(pair, slab_given.at[rows], slab.at[rows])

    loads = {
        "core_cols": load(4, core_cols_given, core_cols),
        "first_cols": load(5, first_cols_given, first_cols),
        "third_cols": load(6, third_cols_given, third_cols),
        "core_frames": load(7, core_frames_given, core_frames),
        "second_rows": load(8, second_rows_given, second_rows),
        "third_rows": load(9, third_rows_given, third_rows),
        "second_frames": load(10, second_frames_given, second_frames),
        "first_frames": load(11, first_frames_given, first_frames),
    }
    loads["core_cols"].start()
    load_pair(0).start()
    loads["core_frames"].start()
    for pair in (1, 2, 3):
        load_pair(pair).start()
    for each in ("first_cols", "third_cols", "second_rows", "third_rows", "second_frames", "first_frames"):
        loads[each].start()

    barrier = pltpu.get_barrier_semaphore()

    def greet(device):
        pl.semaphore_signal(barrier, inc=1, device_id=device, device_id_type=MESH)

    @pl.loop(1, 16)
    def _(step):
        greet((y_hi * 16 + lax.rem(space + step, 16), tm))

    @pl.loop(1, 8)
    def _(step):
        greet(at_y(lax.rem(y + step, 8)))

    greet(((1 - y_hi) * 16 + z * 2 + 1 - core, tm))
    for step in (1, 2, 3):
        greet(at_x(lax.rem(x + step, 4)))

    loads["core_cols"].wait()

    for quarter in range(4):
        lanes = slice(128 * quarter, 128 * quarter + 128)
        order[quarter] = core_cols[:, lanes]
        for half in range(2):
            for place in range(10):
                hi, lo = halves(order[quarter, pl.ds(160 * half + place, 16, stride=10), :])
                base = 256 + 128 * half + 16 * place if place < 8 else 512 + 32 * half + 16 * (place - 8)
                cols_hi[base : base + 16, lanes], cols_lo[base : base + 16, lanes] = hi, lo

    loads["core_frames"].wait()

    for other in range(4):
        for place in range(4):
            base = 12 * (place * 4 + other)
            row = 24 * (other * 4 + place)
            eight = core_frames[base : base + 8, :]
            four = core_frames[base + 8 : base + 12, :]
            blank = jnp.zeros((8, 128), f32)
            blank4 = jnp.zeros((4, 128), f32)
            block = jnp.concatenate(
                [
                    jnp.concatenate([eight, blank], axis=1),
                    jnp.concatenate([blank, eight], axis=1),
                    jnp.concatenate([four, blank4], axis=1),
                    jnp.concatenate([blank4, four], axis=1),
                ],
                axis=0,
            )
            hi, lo = halves(block)
            frames_hi[row : row + 24, :], frames_lo[row : row + 24, :] = hi, lo

    def columns(pair):
        load_pair(pair).wait()
        block = jnp.concatenate([slab[2 * pair], slab[2 * pair + 1]], axis=1)
        hi, lo = halves(block)
        split[:, pair * 256 : pair * 256 + 256] = hi
        split[:, pair * 256 + 1024 : pair * 256 + 1280] = lo
        product = dot(cols_hi[256:576], hi) + dot(cols_hi[256:576], lo) + dot(cols_lo[256:576], hi)
        hi, lo = halves(product[256:320, :].reshape(2, 32, 256))
        rest_hi[:, pair], rest_lo[:, pair] = hi, lo
        frames(pair, *halves(product[0:256, :]))

    def other_columns(pair):
        hi = split[:, pair * 256 : pair * 256 + 256]
        lo = split[:, pair * 256 + 1024 : pair * 256 + 1280]
        inner[pair] = dot(cols_hi[0:256], hi) + dot(cols_hi[0:256], lo) + dot(cols_lo[0:256], hi)

    def frames(unit, right_hi, right_lo):
        product = (
            dot(frames_hi[...], right_hi, NT) + dot(frames_hi[...], right_lo, NT) + dot(frames_lo[...], right_hi, NT)
        )
        for half in range(2):
            part[unit, :, half] = product[:, 128 * half : 128 * half + 128].reshape(4, 4, 24, 128)

    def copy(source, target, number, device):
        return pltpu.make_async_remote_copy(
            src_ref=source, dst_ref=target, send_sem=send_sem.at[number], recv_sem=recv_sem.at[number],
            device_id=device, device_id_type=MESH,
        )

    right, left, across = lax.rem(x + 1, 4), lax.rem(x + 3, 4), lax.rem(x + 2, 4)

    sent = []

    ways = ((right, left), (left, right), (right, left), (left, right), (right, left), (left, right))

    def own(piece, owner):
        return part.at[piece, owner] if piece < 4 else part.at[4, owner, piece - 4]

    def landing(ref, piece):
        return ref.at[piece] if piece < 4 else ref.at[4, piece - 4]

    def far_copy(piece):
        return copy(own(piece, across), landing(far, piece), 3 * piece, at_x(ways[piece][0]))

    def near_copy(piece):
        back = ways[piece][1]
        return copy(own(piece, back), landing(near, piece), 3 * piece + 1, at_x(back))

    def after_copy(piece):
        onward = ways[piece][0]
        return copy(own(piece, onward), landing(after, piece), 3 * piece + 2, at_x(onward))

    def begin(each):
        each.start()
        sent.append(each)

    def relay(piece):
        far_copy(piece).wait_recv()
        if piece < 4:
            part[piece, ways[piece][0]] += far[piece]
        else:
            part[4, ways[piece][0], piece - 4] += far[4, piece - 4]
        begin(after_copy(piece))

    def y_copy(unit, other, slot):
        return pltpu.make_async_remote_copy(
            src_ref=part.at[unit, x, other // 4, lax.rem(other, 4)], dst_ref=line.at[unit, slot],
            send_sem=send_y.at[unit, other], recv_sem=recv_y.at[unit, slot],
            device_id=at_y(other), device_id_type=MESH,
        )

    def y_begin(unit):
        for piece in (unit,) if unit < 4 else (4, 5):
            near_copy(piece).wait_recv()
            after_copy(piece).wait_recv()
        part[unit, x] = part[unit, x] + near[unit] + after[unit]

        for step in (4, 3, 5, 2, 6, 1, 7):
            y_copy(unit, lax.rem(y + step, 8), y).start()

        line[unit, y] = part[unit, x, y_hi, y_lo]

    row = lax.rem(lax.broadcasted_iota(jnp.int32, (48, 256), 0), 24)
    lane = lax.broadcasted_iota(jnp.int32, (48, 256), 1)
    side, lane = lane // 128, lax.rem(lane, 128)
    rank = lax.rem(lane, 12)
    wanted = jnp.where(rank < 8, 8 * side + rank, 8 + 4 * side + rank)
    pick = ((row == wanted) & (lane < 120)).astype(f32).astype(bf16)
    lane_place = lax.broadcasted_iota(jnp.int32, (16, 256), 1)
    lane_place = lax.rem(lane_place, 128) // 12

    def y_end(unit):
        @pl.loop(1, 8)
        def _(step):
            other = lax.rem(y + step, 8)
            y_copy(unit, other, other).wait_recv()

        value = jnp.concatenate([jnp.sum(line[unit, 0:4], axis=0), jnp.sum(line[unit, 4:8], axis=0)], axis=1)
        turned = dot(jnp.concatenate(halves(value), axis=0), pick, TN)
        return turned.reshape(2, 8, 16, 256)

    def tile_rows(half, row):
        return pl.ds(8 * half + row, 16, stride=16)

    def unit_end(unit):
        turned = y_end(unit)
        for half in range(2):
            total = jnp.zeros((16, 256), f32)
            for place in range(8):
                total = jnp.where(lane_place == place, turned[half, place], total)
            for row in range(2):
                tiles[tile_rows(half, 2 * unit + row), :] = total[:, 128 * row : 128 * row + 128]

    def rest_end():
        turned = y_end(4)
        for half in range(2):
            for pair in range(4):
                total = jnp.where(lane_place == 8, turned[half, 2 * pair], turned[half, 2 * pair + 1])
                for row in range(2):
                    rows = tile_rows(half, 2 * pair + row)
                    lanes = slice(128 * row, 128 * row + 128)
                    tiles[rows, :] = jnp.where(lane_place[:, lanes] < 8, tiles[rows, :], total[:, lanes])

    columns(0)
    pl.semaphore_wait(barrier, 26)
    begin(far_copy(0))
    begin(near_copy(0))
    columns(1)
    begin(far_copy(1))
    begin(near_copy(1))
    columns(2)
    begin(far_copy(2))
    columns(3)
    begin(far_copy(3))
    frames(4, rest_hi[...].reshape(256, 256), rest_lo[...].reshape(256, 256))

    loads["first_cols"].wait()
    loads["third_cols"].wait()
    hi, lo = halves(first_cols[...])
    cols_hi[0:160, :], cols_lo[0:160, :] = hi, lo
    hi, lo = halves(third_cols[...])
    cols_hi[160:256, :], cols_lo[160:256, :] = hi, lo
    for pair in range(4):
        other_columns(pair)

    relay(0)
    begin(far_copy(4))
    begin(near_copy(2))

    index_k = lax.broadcasted_iota(jnp.int32, (8, 1024), 0)
    index_l = lax.broadcasted_iota(jnp.int32, (8, 1024), 1) // 128
    spread = (index_k == index_l).astype(f32)

    for each in ("second_rows", "third_rows", "second_frames", "first_frames"):
        loads[each].wait()

    def widen(values):
        return lax.dot_general(values, spread, TN, precision=lax.Precision.HIGHEST, preferred_element_type=f32)

    wide_second = widen(second_rows[...])
    for row in range(8):
        lanes = slice(row * 128, row * 128 + 128)
        value = second_frames[...] * wide_second[:, lanes]
        hi, lo = halves(value)
        second_hi[0:128, lanes], second_lo[0:128, lanes] = hi[0:128], lo[0:128]
        for copies in range(4):
            rows = slice(128 + 32 * copies, 160 + 32 * copies)
            second_hi[rows, lanes], second_lo[rows, lanes] = hi[128:160], lo[128:160]
    third_wide[...] = widen(third_rows[...])

    second = (
        dot(split[:, 0:1024], second_hi[...], NT)
        + dot(split[:, 1024:2048], second_hi[...], NT)
        + dot(split[:, 0:1024], second_lo[...], NT)
    )
    main = second[:, 0:128].reshape(2, 8, 2, 16, 128)
    tail = second[:, 128:256].reshape(2, 8, 2, 2, 8, 128)
    quarter = lax.broadcasted_iota(jnp.int32, (8, 8, 128), 2) // 32
    for which in range(2):
        small[which, :, 0:16, :] = main[0, :, which]
        small[which, :, 16:32, :] = main[1, :, which]
        small[which, :, 32:40, :] = jnp.where(
            quarter < 2,
            jnp.where(quarter == 0, tail[0, :, which, 0], tail[0, :, which, 1]),
            jnp.where(quarter == 2, tail[1, :, which, 0], tail[1, :, which, 1]),
        )

    relay(1)
    begin(far_copy(5))

    total = jnp.zeros((96, 128), f32)
    for row in range(8):
        place = slice((row % 2) * 128, (row % 2) * 128 + 128)
        total = total + inner[row // 2, 160:256, place] * third_wide[:, row * 128 : row * 128 + 128]
    frame_part[...] = total.reshape(2, 2, 24, 128)

    other_core = (y_hi * 16 + z * 2 + 1 - core, tm)
    swap = copy(small.at[1 - core], core_in, 18, other_core)
    swap.start()
    swap_frames = copy(frame_part.at[1 - core], frame_in, 19, other_core)
    swap_frames.start()
    sent.extend([swap, swap_frames])

    relay(2)
    begin(near_copy(3))

    swap.wait_recv()
    layer_out[...] = small[core] + core_in[...]
    swap_frames.wait_recv()
    frame_pair[...] = frame_part[core] + frame_in[...]

    def layer_copy(other, slot):
        return pltpu.make_async_remote_copy(
            src_ref=layer_out.at[other], dst_ref=layer_in.at[slot], send_sem=send_layer.at[0, other],
            recv_sem=recv_layer.at[0, slot], device_id=at_z(other), device_id_type=MESH,
        )

    def frame_copy(other, slot):
        return pltpu.make_async_remote_copy(
            src_ref=frame_layer.at[z], dst_ref=frame_layer.at[slot], send_sem=send_layer.at[1, other],
            recv_sem=recv_layer.at[1, slot], device_id=at_z(other), device_id_type=MESH,
        )

    for step in (4, 3, 5, 2, 6, 1, 7):
        layer_copy(lax.rem(z + step, 8), z).start()
    layer_in[z] = layer_out[z]
    flip = copy(frame_pair.at[1 - y_hi], frame_other, 20, (lax.rem(space + 16, 32), tm))
    begin(flip)

    relay(3)
    y_begin(0)

    rows_total = jnp.zeros((16, 160), f32)
    index_k = lax.broadcasted_iota(jnp.int32, (16, 256), 0)
    index_l = lax.broadcasted_iota(jnp.int32, (16, 256), 1) // 128
    for pair in range(4):
        value = inner[pair, 0:160, :] * jnp.concatenate([first_frames[...], first_frames[...]], axis=1)
        hi, lo = halves(value)
        ones = (index_k == index_l + 2 * pair).astype(f32).astype(bf16)
        rows_total = rows_total + dot(ones, hi, NT) + dot(ones, lo, NT)

    begin(near_copy(5))
    begin(near_copy(4))
    relay(4)
    y_begin(1)
    relay(5)
    y_begin(2)
    y_begin(3)

    flip.wait_recv()
    frame_layer[z] = frame_pair[y_hi] + frame_other[...]
    for step in (4, 3, 5, 2, 6, 1, 7):
        frame_copy(lax.rem(z + step, 8), z).start()

    @pl.loop(1, 8)
    def _(step):
        other = lax.rem(z + step, 8)
        layer_copy(other, other).wait_recv()

    line_out[0:40, :] = jnp.sum(layer_in[...], axis=0)
    line_out[40:48, :] = jnp.zeros((8, 128), f32)
    line_out[48:56, :] = rows_total[0:8, 0:128]
    line_out[56:64, :] = jnp.concatenate([rows_total[0:8, 128:160], jnp.zeros((8, 96), f32)], axis=1)

    def line_copy(other, slot):
        return pltpu.make_async_remote_copy(
            src_ref=line_out.at[pl.ds(pl.multiple_of(other * 16, 16), 16)], dst_ref=line_in.at[slot],
            send_sem=send_line.at[other], recv_sem=recv_line.at[slot],
            device_id=at_x(other), device_id_type=MESH,
        )

    for step in (2, 1, 3):
        line_copy(lax.rem(x + step, 4), x).start()
    line_in[x] = line_out[pl.ds(pl.multiple_of(x * 16, 16), 16)]

    y_begin(4)
    unit_end(0)
    unit_end(1)
    unit_end(2)

    for step in (1, 2, 3):
        other = lax.rem(x + step, 4)
        line_copy(other, other).wait_recv()
    ring_in[y] = jnp.sum(line_in[...], axis=0)

    def ring_copy(other, slot):
        return pltpu.make_async_remote_copy(
            src_ref=ring_in.at[y], dst_ref=ring_in.at[slot], send_sem=send_ring.at[other], recv_sem=recv_ring.at[slot],
            device_id=at_y(other), device_id_type=MESH,
        )

    for step in (4, 3, 5, 2, 6, 1, 7):
        ring_copy(lax.rem(y + step, 8), y).start()

    unit_end(3)

    @pl.loop(1, 8)
    def _(step):
        other = lax.rem(z + step, 8)
        frame_copy(other, other).wait_recv()

    frame_sums[core, y_hi] = jnp.sum(frame_layer[...], axis=0)

    def quarter_copy(device_core, device_half, slot_core, slot_half):
        return pltpu.make_async_remote_copy(
            src_ref=frame_sums.at[core, y_hi], dst_ref=frame_sums.at[slot_core, slot_half],
            send_sem=send_quarter.at[device_core, device_half], recv_sem=recv_quarter.at[slot_core, slot_half],
            device_id=(device_half * 16 + z * 2 + device_core, tm), device_id_type=MESH,
        )

    others = ((core, 1 - y_hi), (1 - core, 1 - y_hi), (1 - core, y_hi))
    for other in others:
        begin(quarter_copy(*other, core, y_hi))

    rest_end()

    mine = lax.rem(space, 16)
    tile_view = tiles.reshape(16, 2, 8, 128)

    def tile_copy(other, slot):
        return pltpu.make_async_remote_copy(
            src_ref=tile_view.at[other], dst_ref=gathered.at[:, slot],
            send_sem=send_space.at[other], recv_sem=recv_space.at[slot],
            device_id=(y_hi * 16 + other, tm), device_id_type=MESH,
        )

    for step in (8, 7, 9, 6, 10, 5, 11, 4, 12, 3, 13, 2, 14, 1, 15):
        tile_copy(lax.rem(mine + step, 16), mine).start()

    keep = load(0, tile_view.at[mine], gathered.at[:, mine])
    keep.start()

    @pl.loop(1, 8)
    def _(step):
        other = lax.rem(y + step, 8)
        ring_copy(other, other).wait_recv()

    half_sum = jnp.sum(ring_in[pl.ds(y_hi * 4, 4)], axis=0)
    piece_in[x] = jnp.where(x == 3, half_sum, jnp.sum(ring_in[...], axis=0))

    def piece_copy(other, slot):
        return pltpu.make_async_remote_copy(
            src_ref=piece_in.at[x], dst_ref=piece_in.at[slot], send_sem=send_piece.at[other], recv_sem=recv_piece.at[slot],
            device_id=at_x(other), device_id_type=MESH,
        )

    for step in (2, 1, 3):
        piece_copy(lax.rem(x + step, 4), x).start()

    for each in sent:
        each.wait_send()

    @pl.loop(1, 8)
    def _(step):
        other = lax.rem(z + step, 8)
        layer_copy(other, z).wait_send()
        frame_copy(other, z).wait_send()
        other = lax.rem(y + step, 8)
        ring_copy(other, y).wait_send()
        for unit in range(5):
            y_copy(unit, other, y).wait_send()

    for step in (1, 2, 3):
        other = lax.rem(x + step, 4)
        line_copy(other, x).wait_send()
        piece_copy(other, x).wait_send()

    @pl.loop(1, 16)
    def _(step):
        tile_copy(lax.rem(mine + step, 16), mine).wait_send()

    for step in (1, 2, 3):
        other = lax.rem(x + step, 4)
        piece_copy(other, other).wait_recv()
    small_sums[0:16, :] = piece_in[y_hi]
    small_sums[16:24, :] = piece_in[2, 0:8]

    @pl.when(y_hi == 1)
    def _():
        small_sums[16:24, 0:64] = piece_in[2, 0:8, 64:128]

    small_sums[24:40, :] = piece_in[3]
    keep_small = load(1, small_sums, out_small)
    keep_small.start()
    for other in others:
        quarter_copy(*other, *other).wait_recv()
    keep_frames = load(2, frame_sums, out_frames)
    keep_frames.start()

    @pl.loop(1, 16)
    def _(step):
        other = lax.rem(mine + step, 16)
        tile_copy(other, other).wait_recv()

    for each in (keep, keep_small, keep_frames):
        each.wait()


def finish(gathered, small, frames, core_rows, out_rows, out_cols, out_frames, out_core):
    out_rows[:, 0:128] = small[24:32, :]
    out_rows[:, 128:160] = small[32:40, 0:32]
    out_cols[:, 0:128] = small[0:16, :]
    for half in range(2):
        out_cols[8 * half : 8 * half + 8, 128:160] = small[16:24, 32 * half : 32 * half + 32]
    out_frames[...] = frames[...]
    hi, lo = halves(gathered[...].reshape(256, 128).T)
    rows_hi, rows_lo = halves(core_rows[...])
    result = dot(hi, rows_hi, NT) + dot(hi, rows_lo, NT) + dot(lo, rows_hi, NT)
    for place in range(10):
        out_core[place] = result[12 * place : 12 * place + 12]


def per_device(
    video_slab, first_cols, first_frames, second_rows, second_frames, third_rows, third_cols, core_rows, core_cols, core_frames,
):
    arguments = (
        video_slab, first_cols.T, third_cols.T, core_cols.T, first_frames.T, second_frames.T, core_frames.T,
        second_rows, third_rows,
    )
    vmem = pl.BlockSpec(memory_space=pltpu.VMEM)
    dma = pltpu.SemaphoreType.DMA
    scratch = [pltpu.VMEM((40, 128), f32), pltpu.VMEM((2, 2, 24, 128), f32)]
    scratch += [pltpu.VMEM(each.shape, f32) for each in arguments] + [
        pltpu.VMEM((4, 320, 128), f32),
        pltpu.VMEM((576, 512), bf16), pltpu.VMEM((576, 512), bf16),
        pltpu.VMEM((384, 256), bf16), pltpu.VMEM((384, 256), bf16),
        pltpu.VMEM((512, 2048), bf16),
        pltpu.VMEM((4, 256, 256), f32),
        pltpu.VMEM((2, 4, 32, 256), bf16), pltpu.VMEM((2, 4, 32, 256), bf16),
        pltpu.VMEM((256, 1024), bf16), pltpu.VMEM((256, 1024), bf16),
        pltpu.VMEM((96, 1024), f32),
        pltpu.VMEM((5, 4, 2, 4, 24, 128), f32), *[pltpu.VMEM((5, 2, 4, 24, 128), f32)] * 3,
        pltpu.VMEM((5, 8, 24, 128), f32),
        pltpu.VMEM((256, 128), f32),
        pltpu.VMEM((2, 8, 40, 128), f32), pltpu.VMEM((8, 40, 128), f32),
        pltpu.VMEM((8, 40, 128), f32), pltpu.VMEM((8, 40, 128), f32),
        pltpu.VMEM((2, 2, 24, 128), f32), pltpu.VMEM((2, 24, 128), f32), pltpu.VMEM((2, 24, 128), f32),
        pltpu.VMEM((24, 128), f32), pltpu.VMEM((8, 24, 128), f32),
        pltpu.VMEM((64, 128), f32), pltpu.VMEM((4, 16, 128), f32), pltpu.VMEM((8, 16, 128), f32), pltpu.VMEM((4, 16, 128), f32),
        dma((12,)), dma((22,)), dma((22,)), dma((16,)), dma((16,)), dma((2, 8)), dma((2, 8)), dma((4,)), dma((4,)), dma((8,)), dma((8,)), dma((5, 8)), dma((5, 8)),
        dma((4,)), dma((4,)), dma((2, 2)), dma((2, 2)),
    ]
    gathered, small, frames = pl.pallas_call(
        kernel,
        out_shape=[
            jax.ShapeDtypeStruct((2, 16, 8, 128), f32),
            jax.ShapeDtypeStruct((40, 128), f32),
            jax.ShapeDtypeStruct((2, 2, 24, 128), f32),
        ],
        in_specs=[pl.BlockSpec(memory_space=pltpu.HBM)] * 9,
        out_specs=[pl.BlockSpec(memory_space=pltpu.HBM)] * 3,
        scratch_shapes=scratch,
        compiler_params=pltpu.CompilerParams(collective_id=0, has_side_effects=True, vmem_limit_bytes=60 * 2**20),
    )(*arguments)
    rows, cols, frames, core = pl.pallas_call(
        finish,
        out_shape=[
            jax.ShapeDtypeStruct((8, 160), f32),
            jax.ShapeDtypeStruct((16, 160), f32),
            jax.ShapeDtypeStruct((2, 2, 24, 128), f32),
            jax.ShapeDtypeStruct((10, 12, 320), f32),
        ],
        in_specs=[vmem] * 4,
        out_specs=[vmem] * 4,
        compiler_params=pltpu.CompilerParams(vmem_limit_bytes=60 * 2**20),
    )(gathered, small, frames, core_rows.T)
    return rows, cols, frames.reshape(96, 128).T, core.transpose(2, 0, 1)


def solution(mesh):
    return jax.shard_map(
        per_device,
        mesh=mesh,
        in_specs=(
            P("space", None, "tm"),
            P(),
            P("tm", None),
            P("space", None),
            P("tm", None),
            P("space", None),
            P(),
            P(),
            P(),
            P("tm", None),
        ),
        out_specs=(P("space", None), P("space", None), P("tm", None), P(None, "space", "tm")),
        check_vma=False,
    )
```

```python
import functools

import jax
import jax.numpy as jnp
from jax import lax
from jax.experimental import pallas as pl
from jax.experimental.pallas import tpu as pltpu
from jax.sharding import PartitionSpec as P

MESH = pl.DeviceIdType.MESH
f32, bf16 = jnp.float32, jnp.bfloat16

NN = (((1,), (0,)), ((), ()))
NT = (((1,), (1,)), ((), ()))
TN = (((0,), (0,)), ((), ()))


def dot(a, b, dims=NN):
    return lax.dot_general(a, b, dims, preferred_element_type=f32)


def halves(a):
    high = a.astype(bf16)
    return high, (a - high.astype(f32)).astype(bf16)


def kernel(
    slab_given, first_cols_given, third_cols_given, core_cols_given, first_frames_given, second_frames_given,
    core_frames_given, second_rows_given, third_rows_given,
    gathered, out_small, out_frames,
    small_sums, frame_sums,
    slab, first_cols, third_cols, core_cols, first_frames, second_frames, core_frames, second_rows, third_rows,
    order, cols_hi, cols_lo, frames_hi, frames_lo, split, inner, rest_hi, rest_lo, second_hi, second_lo, third_wide,
    part, far, near, after, line, tiles,
    small, core_in, layer_out, layer_in, frame_part, frame_in, frame_pair, frame_other, frame_layer,
    line_out, line_in, ring_in, piece_in,
    load_sem, send_sem, recv_sem, send_space, recv_space, send_layer, recv_layer, send_line, recv_line, send_ring, recv_ring, send_y, recv_y,
    send_piece, recv_piece, send_quarter, recv_quarter,
):
    space, tm = lax.axis_index("space"), lax.axis_index("tm")
    y_hi, z, core = space // 16, lax.rem(space // 2, 8), lax.rem(space, 2)
    y_lo, x = tm // 4, lax.rem(tm, 4)
    y = y_hi * 4 + y_lo

    def at_x(other):
        return (space, y_lo * 4 + other)

    def at_y(other):
        return (lax.rem(other // 4, 2) * 16 + z * 2 + core, lax.rem(other, 4) * 4 + x)

    def at_z(other):
        return (y_hi * 16 + other * 2 + core, tm)

    def load(number, source, target):
        return pltpu.make_async_copy(source, target, load_sem.at[number])

    def load_pair(pair):
        rows = pl.ds(2 * pair, 2)
        return load(pair, slab_given.at[rows], slab.at[rows])

    loads = {
        "core_cols": load(4, core_cols_given, core_cols),
        "first_cols": load(5, first_cols_given, first_cols),
        "third_cols": load(6, third_cols_given, third_cols),
        "core_frames": load(7, core_frames_given, core_frames),
        "second_rows": load(8, second_rows_given, second_rows),
        "third_rows": load(9, third_rows_given, third_rows),
        "second_frames": load(10, second_frames_given, second_frames),
        "first_frames": load(11, first_frames_given, first_frames),
    }
    loads["core_cols"].start()
    load_pair(0).start()
    loads["core_frames"].start()
    for pair in (1, 2, 3):
        load_pair(pair).start()
    for each in ("first_cols", "third_cols", "second_rows", "third_rows", "second_frames", "first_frames"):
        loads[each].start()

    barrier = pltpu.get_barrier_semaphore()

    def greet(device):
        pl.semaphore_signal(barrier, inc=1, device_id=device, device_id_type=MESH)

    @pl.loop(1, 16)
    def _(step):
        greet((y_hi * 16 + lax.rem(space + step, 16), tm))

    @pl.loop(1, 8)
    def _(step):
        greet(at_y(lax.rem(y + step, 8)))

    greet(((1 - y_hi) * 16 + z * 2 + 1 - core, tm))
    for step in (1, 2, 3):
        greet(at_x(lax.rem(x + step, 4)))

    loads["core_cols"].wait()

    for quarter in range(4):
        lanes = slice(128 * quarter, 128 * quarter + 128)
        order[quarter] = core_cols[:, lanes]
        for half in range(2):
            for place in range(10):
                hi, lo = halves(order[quarter, pl.ds(160 * half + place, 16, stride=10), :])
                base = 256 + 128 * half + 16 * place if place < 8 else 512 + 32 * half + 16 * (place - 8)
                cols_hi[base : base + 16, lanes], cols_lo[base : base + 16, lanes] = hi, lo

    loads["core_frames"].wait()

    for other in range(4):
        for place in range(4):
            base = 12 * (place * 4 + other)
            row = 24 * (other * 4 + place)
            eight = core_frames[base : base + 8, :]
            four = core_frames[base + 8 : base + 12, :]
            blank = jnp.zeros((8, 128), f32)
            blank4 = jnp.zeros((4, 128), f32)
            block = jnp.concatenate(
                [
                    jnp.concatenate([eight, blank], axis=1),
                    jnp.concatenate([blank, eight], axis=1),
                    jnp.concatenate([four, blank4], axis=1),
                    jnp.concatenate([blank4, four], axis=1),
                ],
                axis=0,
            )
            hi, lo = halves(block)
            frames_hi[row : row + 24, :], frames_lo[row : row + 24, :] = hi, lo

    def columns(pair):
        load_pair(pair).wait()
        block = jnp.concatenate([slab[2 * pair], slab[2 * pair + 1]], axis=1)
        hi, lo = halves(block)
        split[:, pair * 256 : pair * 256 + 256] = hi
        split[:, pair * 256 + 1024 : pair * 256 + 1280] = lo
        product = dot(cols_hi[256:576], hi) + dot(cols_hi[256:576], lo) + dot(cols_lo[256:576], hi)
        hi, lo = halves(product[256:320, :].reshape(2, 32, 256))
        rest_hi[:, pair], rest_lo[:, pair] = hi, lo
        frames(pair, *halves(product[0:256, :]))

    def other_columns(pair):
        hi = split[:, pair * 256 : pair * 256 + 256]
        lo = split[:, pair * 256 + 1024 : pair * 256 + 1280]
        inner[pair] = dot(cols_hi[0:256], hi) + dot(cols_hi[0:256], lo) + dot(cols_lo[0:256], hi)

    def frames(unit, right_hi, right_lo):
        product = (
            dot(frames_hi[...], right_hi, NT) + dot(frames_hi[...], right_lo, NT) + dot(frames_lo[...], right_hi, NT)
        )
        for half in range(2):
            part[unit, :, half] = product[:, 128 * half : 128 * half + 128].reshape(4, 4, 24, 128)

    def copy(source, target, number, device):
        return pltpu.make_async_remote_copy(
            src_ref=source, dst_ref=target, send_sem=send_sem.at[number], recv_sem=recv_sem.at[number],
            device_id=device, device_id_type=MESH,
        )

    right, left, across = lax.rem(x + 1, 4), lax.rem(x + 3, 4), lax.rem(x + 2, 4)

    sent = []

    ways = ((right, left), (left, right), (right, left), (left, right), (right, left), (left, right))

    def own(piece, owner):
        return part.at[piece, owner] if piece < 4 else part.at[4, owner, piece - 4]

    def landing(ref, piece):
        return ref.at[piece] if piece < 4 else ref.at[4, piece - 4]

    def far_copy(piece):
        return copy(own(piece, across), landing(far, piece), 3 * piece, at_x(ways[piece][0]))

    def near_copy(piece):
        back = ways[piece][1]
        return copy(own(piece, back), landing(near, piece), 3 * piece + 1, at_x(back))

    def after_copy(piece):
        onward = ways[piece][0]
        return copy(own(piece, onward), landing(after, piece), 3 * piece + 2, at_x(onward))

    def begin(each):
        each.start()
        sent.append(each)

    def relay(piece):
        far_copy(piece).wait_recv()
        if piece < 4:
            part[piece, ways[piece][0]] += far[piece]
        else:
            part[4, ways[piece][0], piece - 4] += far[4, piece - 4]
        begin(after_copy(piece))

    def y_copy(unit, other, slot):
        return pltpu.make_async_remote_copy(
            src_ref=part.at[unit, x, other // 4, lax.rem(other, 4)], dst_ref=line.at[unit, slot],
            send_sem=send_y.at[unit, other], recv_sem=recv_y.at[unit],
            device_id=at_y(other), device_id_type=MESH,
        )

    def y_begin(unit):
        for piece in (unit,) if unit < 4 else (4, 5):
            near_copy(piece).wait_recv()
            after_copy(piece).wait_recv()
        part[unit, x] = part[unit, x] + near[unit] + after[unit]

        for step in (4, 3, 5, 2, 6, 1, 7):
            y_copy(unit, lax.rem(y + step, 8), y).start()

        line[unit, y] = part[unit, x, y_hi, y_lo]

    row = lax.rem(lax.broadcasted_iota(jnp.int32, (48, 256), 0), 24)
    lane = lax.broadcasted_iota(jnp.int32, (48, 256), 1)
    side, lane = lane // 128, lax.rem(lane, 128)
    rank = lax.rem(lane, 12)
    wanted = jnp.where(rank < 8, 8 * side + rank, 8 + 4 * side + rank)
    pick = ((row == wanted) & (lane < 120)).astype(f32).astype(bf16)
    lane_place = lax.broadcasted_iota(jnp.int32, (16, 256), 1)
    lane_place = lax.rem(lane_place, 128) // 12

    def y_end(unit):
        all_seven = line.at[unit, pl.ds(0, 7)]
        pltpu.make_async_copy(all_seven, all_seven, recv_y.at[unit]).wait()
        value = jnp.concatenate([jnp.sum(line[unit, 0:4], axis=0), jnp.sum(line[unit, 4:8], axis=0)], axis=1)
        turned = dot(jnp.concatenate(halves(value), axis=0), pick, TN)
        return turned.reshape(2, 8, 16, 256)

    def tile_rows(half, row):
        return pl.ds(8 * half + row, 16, stride=16)

    def unit_end(unit):
        turned = y_end(unit)
        for half in range(2):
            total = jnp.zeros((16, 256), f32)
            for place in range(8):
                total = jnp.where(lane_place == place, turned[half, place], total)
            for row in range(2):
                tiles[tile_rows(half, 2 * unit + row), :] = total[:, 128 * row : 128 * row + 128]

    def rest_end():
        turned = y_end(4)
        for half in range(2):
            for pair in range(4):
                total = jnp.where(lane_place == 8, turned[half, 2 * pair], turned[half, 2 * pair + 1])
                for row in range(2):
                    rows = tile_rows(half, 2 * pair + row)
                    lanes = slice(128 * row, 128 * row + 128)
                    tiles[rows, :] = jnp.where(lane_place[:, lanes] < 8, tiles[rows, :], total[:, lanes])

    columns(0)
    pl.semaphore_wait(barrier, 26)
    begin(far_copy(0))
    begin(near_copy(0))
    columns(1)
    begin(far_copy(1))
    begin(near_copy(1))
    columns(2)
    begin(far_copy(2))
    columns(3)
    begin(far_copy(3))
    frames(4, rest_hi[...].reshape(256, 256), rest_lo[...].reshape(256, 256))

    loads["first_cols"].wait()
    loads["third_cols"].wait()
    hi, lo = halves(first_cols[...])
    cols_hi[0:160, :], cols_lo[0:160, :] = hi, lo
    hi, lo = halves(third_cols[...])
    cols_hi[160:256, :], cols_lo[160:256, :] = hi, lo
    for pair in range(4):
        other_columns(pair)

    relay(0)
    begin(far_copy(4))
    begin(near_copy(2))

    index_k = lax.broadcasted_iota(jnp.int32, (8, 1024), 0)
    index_l = lax.broadcasted_iota(jnp.int32, (8, 1024), 1) // 128
    spread = (index_k == index_l).astype(f32)

    for each in ("second_rows", "third_rows", "second_frames", "first_frames"):
        loads[each].wait()

    def widen(values):
        return lax.dot_general(values, spread, TN, precision=lax.Precision.HIGHEST, preferred_element_type=f32)

    wide_second = widen(second_rows[...])
    for row in range(8):
        lanes = slice(row * 128, row * 128 + 128)
        value = second_frames[...] * wide_second[:, lanes]
        hi, lo = halves(value)
        second_hi[0:128, lanes], second_lo[0:128, lanes] = hi[0:128], lo[0:128]
        for copies in range(4):
            rows = slice(128 + 32 * copies, 160 + 32 * copies)
            second_hi[rows, lanes], second_lo[rows, lanes] = hi[128:160], lo[128:160]
    third_wide[...] = widen(third_rows[...])

    second = (
        dot(split[:, 0:1024], second_hi[...], NT)
        + dot(split[:, 1024:2048], second_hi[...], NT)
        + dot(split[:, 0:1024], second_lo[...], NT)
    )
    main = second[:, 0:128].reshape(2, 8, 2, 16, 128)
    tail = second[:, 128:256].reshape(2, 8, 2, 2, 8, 128)
    quarter = lax.broadcasted_iota(jnp.int32, (8, 8, 128), 2) // 32
    for which in range(2):
        small[which, :, 0:16, :] = main[0, :, which]
        small[which, :, 16:32, :] = main[1, :, which]
        small[which, :, 32:40, :] = jnp.where(
            quarter < 2,
            jnp.where(quarter == 0, tail[0, :, which, 0], tail[0, :, which, 1]),
            jnp.where(quarter == 2, tail[1, :, which, 0], tail[1, :, which, 1]),
        )

    relay(1)
    begin(far_copy(5))

    total = jnp.zeros((96, 128), f32)
    for row in range(8):
        place = slice((row % 2) * 128, (row % 2) * 128 + 128)
        total = total + inner[row // 2, 160:256, place] * third_wide[:, row * 128 : row * 128 + 128]
    frame_part[...] = total.reshape(2, 2, 24, 128)

    other_core = (y_hi * 16 + z * 2 + 1 - core, tm)
    swap = copy(small.at[1 - core], core_in, 18, other_core)
    swap.start()
    swap_frames = copy(frame_part.at[1 - core], frame_in, 19, other_core)
    swap_frames.start()
    sent.extend([swap, swap_frames])

    relay(2)
    begin(near_copy(3))

    swap.wait_recv()
    layer_out[...] = small[core] + core_in[...]
    swap_frames.wait_recv()
    frame_pair[...] = frame_part[core] + frame_in[...]

    def layer_copy(other, slot):
        return pltpu.make_async_remote_copy(
            src_ref=layer_out.at[other], dst_ref=layer_in.at[slot], send_sem=send_layer.at[0, other],
            recv_sem=recv_layer.at[0, slot], device_id=at_z(other), device_id_type=MESH,
        )

    def frame_copy(other, slot):
        return pltpu.make_async_remote_copy(
            src_ref=frame_layer.at[z], dst_ref=frame_layer.at[slot], send_sem=send_layer.at[1, other],
            recv_sem=recv_layer.at[1, slot], device_id=at_z(other), device_id_type=MESH,
        )

    for step in (4, 3, 5, 2, 6, 1, 7):
        layer_copy(lax.rem(z + step, 8), z).start()
    layer_in[z] = layer_out[z]
    flip = copy(frame_pair.at[1 - y_hi], frame_other, 20, (lax.rem(space + 16, 32), tm))
    begin(flip)

    relay(3)
    y_begin(0)

    rows_total = jnp.zeros((16, 160), f32)
    index_k = lax.broadcasted_iota(jnp.int32, (16, 256), 0)
    index_l = lax.broadcasted_iota(jnp.int32, (16, 256), 1) // 128
    for pair in range(4):
        value = inner[pair, 0:160, :] * jnp.concatenate([first_frames[...], first_frames[...]], axis=1)
        hi, lo = halves(value)
        ones = (index_k == index_l + 2 * pair).astype(f32).astype(bf16)
        rows_total = rows_total + dot(ones, hi, NT) + dot(ones, lo, NT)

    begin(near_copy(5))
    begin(near_copy(4))
    relay(4)
    y_begin(1)
    relay(5)
    y_begin(2)
    y_begin(3)

    flip.wait_recv()
    frame_layer[z] = frame_pair[y_hi] + frame_other[...]
    for step in (4, 3, 5, 2, 6, 1, 7):
        frame_copy(lax.rem(z + step, 8), z).start()

    @pl.loop(1, 8)
    def _(step):
        other = lax.rem(z + step, 8)
        layer_copy(other, other).wait_recv()

    line_out[0:40, :] = jnp.sum(layer_in[...], axis=0)
    line_out[40:48, :] = jnp.zeros((8, 128), f32)
    line_out[48:56, :] = rows_total[0:8, 0:128]
    line_out[56:64, :] = jnp.concatenate([rows_total[0:8, 128:160], jnp.zeros((8, 96), f32)], axis=1)

    def line_copy(other, slot):
        return pltpu.make_async_remote_copy(
            src_ref=line_out.at[pl.ds(pl.multiple_of(other * 16, 16), 16)], dst_ref=line_in.at[slot],
            send_sem=send_line.at[other], recv_sem=recv_line.at[slot],
            device_id=at_x(other), device_id_type=MESH,
        )

    for step in (2, 1, 3):
        line_copy(lax.rem(x + step, 4), x).start()
    line_in[x] = line_out[pl.ds(pl.multiple_of(x * 16, 16), 16)]

    y_begin(4)
    unit_end(0)
    unit_end(1)
    unit_end(2)

    for step in (1, 2, 3):
        other = lax.rem(x + step, 4)
        line_copy(other, other).wait_recv()
    ring_in[y] = jnp.sum(line_in[...], axis=0)

    def ring_copy(other, slot):
        return pltpu.make_async_remote_copy(
            src_ref=ring_in.at[y], dst_ref=ring_in.at[slot], send_sem=send_ring.at[other], recv_sem=recv_ring.at[slot],
            device_id=at_y(other), device_id_type=MESH,
        )

    for step in (4, 3, 5, 2, 6, 1, 7):
        ring_copy(lax.rem(y + step, 8), y).start()

    unit_end(3)

    @pl.loop(1, 8)
    def _(step):
        other = lax.rem(z + step, 8)
        frame_copy(other, other).wait_recv()

    frame_sums[core, y_hi] = jnp.sum(frame_layer[...], axis=0)

    def quarter_copy(device_core, device_half, slot_core, slot_half):
        return pltpu.make_async_remote_copy(
            src_ref=frame_sums.at[core, y_hi], dst_ref=frame_sums.at[slot_core, slot_half],
            send_sem=send_quarter.at[device_core, device_half], recv_sem=recv_quarter.at[slot_core, slot_half],
            device_id=(device_half * 16 + z * 2 + device_core, tm), device_id_type=MESH,
        )

    others = ((core, 1 - y_hi), (1 - core, 1 - y_hi), (1 - core, y_hi))
    for other in others:
        begin(quarter_copy(*other, core, y_hi))

    rest_end()

    mine = lax.rem(space, 16)
    tile_view = tiles.reshape(16, 2, 8, 128)

    def tile_copy(other, slot):
        return pltpu.make_async_remote_copy(
            src_ref=tile_view.at[other], dst_ref=gathered.at[:, slot],
            send_sem=send_space.at[other], recv_sem=recv_space.at[0],
            device_id=(y_hi * 16 + other, tm), device_id_type=MESH,
        )

    for step in (8, 7, 9, 6, 10, 5, 11, 4, 12, 3, 13, 2, 14, 1, 15):
        tile_copy(lax.rem(mine + step, 16), mine).start()

    keep = load(0, tile_view.at[mine], gathered.at[:, mine])
    keep.start()

    @pl.loop(1, 8)
    def _(step):
        other = lax.rem(y + step, 8)
        ring_copy(other, other).wait_recv()

    half_sum = jnp.sum(ring_in[pl.ds(y_hi * 4, 4)], axis=0)
    piece_in[x] = jnp.where(x == 3, half_sum, jnp.sum(ring_in[...], axis=0))

    def piece_copy(other, slot):
        return pltpu.make_async_remote_copy(
            src_ref=piece_in.at[x], dst_ref=piece_in.at[slot], send_sem=send_piece.at[other], recv_sem=recv_piece.at[slot],
            device_id=at_x(other), device_id_type=MESH,
        )

    for step in (2, 1, 3):
        piece_copy(lax.rem(x + step, 4), x).start()

    for each in sent:
        each.wait_send()

    @pl.loop(1, 8)
    def _(step):
        other = lax.rem(z + step, 8)
        layer_copy(other, z).wait_send()
        frame_copy(other, z).wait_send()
        other = lax.rem(y + step, 8)
        ring_copy(other, y).wait_send()
        for unit in range(5):
            y_copy(unit, other, y).wait_send()

    for step in (1, 2, 3):
        other = lax.rem(x + step, 4)
        line_copy(other, x).wait_send()
        piece_copy(other, x).wait_send()

    @pl.loop(1, 16)
    def _(step):
        tile_copy(lax.rem(mine + step, 16), mine).wait_send()

    for step in (1, 2, 3):
        other = lax.rem(x + step, 4)
        piece_copy(other, other).wait_recv()
    small_sums[0:16, :] = piece_in[y_hi]
    small_sums[16:24, :] = piece_in[2, 0:8]

    @pl.when(y_hi == 1)
    def _():
        small_sums[16:24, 0:64] = piece_in[2, 0:8, 64:128]

    small_sums[24:40, :] = piece_in[3]
    keep_small = load(1, small_sums, out_small)
    keep_small.start()
    for other in others:
        quarter_copy(*other, *other).wait_recv()
    keep_frames = load(2, frame_sums, out_frames)
    keep_frames.start()

    all_fifteen = gathered.at[:, pl.ds(0, 15)]
    pltpu.make_async_copy(all_fifteen, all_fifteen, recv_space.at[0]).wait()

    for each in (keep, keep_small, keep_frames):
        each.wait()


def finish(gathered, small, frames, core_rows, out_rows, out_cols, out_frames, out_core):
    out_rows[:, 0:128] = small[24:32, :]
    out_rows[:, 128:160] = small[32:40, 0:32]
    out_cols[:, 0:128] = small[0:16, :]
    for half in range(2):
        out_cols[8 * half : 8 * half + 8, 128:160] = small[16:24, 32 * half : 32 * half + 32]
    out_frames[...] = frames[...]
    hi, lo = halves(gathered[...].reshape(256, 128).T)
    rows_hi, rows_lo = halves(core_rows[...])
    result = dot(hi, rows_hi, NT) + dot(hi, rows_lo, NT) + dot(lo, rows_hi, NT)
    for place in range(10):
        out_core[place] = result[12 * place : 12 * place + 12]


def per_device(
    video_slab, first_cols, first_frames, second_rows, second_frames, third_rows, third_cols, core_rows, core_cols, core_frames,
):
    arguments = (
        video_slab, first_cols.T, third_cols.T, core_cols.T, first_frames.T, second_frames.T, core_frames.T,
        second_rows, third_rows,
    )
    vmem = pl.BlockSpec(memory_space=pltpu.VMEM)
    dma = pltpu.SemaphoreType.DMA
    scratch = [pltpu.VMEM((40, 128), f32), pltpu.VMEM((2, 2, 24, 128), f32)]
    scratch += [pltpu.VMEM(each.shape, f32) for each in arguments] + [
        pltpu.VMEM((4, 320, 128), f32),
        pltpu.VMEM((576, 512), bf16), pltpu.VMEM((576, 512), bf16),
        pltpu.VMEM((384, 256), bf16), pltpu.VMEM((384, 256), bf16),
        pltpu.VMEM((512, 2048), bf16),
        pltpu.VMEM((4, 256, 256), f32),
        pltpu.VMEM((2, 4, 32, 256), bf16), pltpu.VMEM((2, 4, 32, 256), bf16),
        pltpu.VMEM((256, 1024), bf16), pltpu.VMEM((256, 1024), bf16),
        pltpu.VMEM((96, 1024), f32),
        pltpu.VMEM((5, 4, 2, 4, 24, 128), f32), *[pltpu.VMEM((5, 2, 4, 24, 128), f32)] * 3,
        pltpu.VMEM((5, 8, 24, 128), f32),
        pltpu.VMEM((256, 128), f32),
        pltpu.VMEM((2, 8, 40, 128), f32), pltpu.VMEM((8, 40, 128), f32),
        pltpu.VMEM((8, 40, 128), f32), pltpu.VMEM((8, 40, 128), f32),
        pltpu.VMEM((2, 2, 24, 128), f32), pltpu.VMEM((2, 24, 128), f32), pltpu.VMEM((2, 24, 128), f32),
        pltpu.VMEM((24, 128), f32), pltpu.VMEM((8, 24, 128), f32),
        pltpu.VMEM((64, 128), f32), pltpu.VMEM((4, 16, 128), f32), pltpu.VMEM((8, 16, 128), f32), pltpu.VMEM((4, 16, 128), f32),
        dma((12,)), dma((22,)), dma((22,)), dma((16,)), dma((1,)), dma((2, 8)), dma((2, 8)), dma((4,)), dma((4,)), dma((8,)), dma((8,)), dma((5, 8)), dma((5,)),
        dma((4,)), dma((4,)), dma((2, 2)), dma((2, 2)),
    ]
    gathered, small, frames = pl.pallas_call(
        kernel,
        out_shape=[
            jax.ShapeDtypeStruct((2, 16, 8, 128), f32),
            jax.ShapeDtypeStruct((40, 128), f32),
            jax.ShapeDtypeStruct((2, 2, 24, 128), f32),
        ],
        in_specs=[pl.BlockSpec(memory_space=pltpu.HBM)] * 9,
        out_specs=[pl.BlockSpec(memory_space=pltpu.HBM)] * 3,
        scratch_shapes=scratch,
        compiler_params=pltpu.CompilerParams(collective_id=0, has_side_effects=True, vmem_limit_bytes=60 * 2**20),
    )(*arguments)
    rows, cols, frames, core = pl.pallas_call(
        finish,
        out_shape=[
            jax.ShapeDtypeStruct((8, 160), f32),
            jax.ShapeDtypeStruct((16, 160), f32),
            jax.ShapeDtypeStruct((2, 2, 24, 128), f32),
            jax.ShapeDtypeStruct((10, 12, 320), f32),
        ],
        in_specs=[vmem] * 4,
        out_specs=[vmem] * 4,
        compiler_params=pltpu.CompilerParams(vmem_limit_bytes=60 * 2**20),
    )(gathered, small, frames, core_rows.T)
    return rows, cols, frames.reshape(96, 128).T, core.transpose(2, 0, 1)


def solution(mesh):
    return jax.shard_map(
        per_device,
        mesh=mesh,
        in_specs=(
            P("space", None, "tm"),
            P(),
            P("tm", None),
            P("space", None),
            P("tm", None),
            P("space", None),
            P(),
            P(),
            P(),
            P("tm", None),
        ),
        out_specs=(P("space", None), P("space", None), P("tm", None), P(None, "space", "tm")),
        check_vma=False,
    )
```
